128 devices in a mesh: atm: 8 (over y, core), ocn: 16 (over z, x).
Axes of the slice: x: 4, y: 4, z: 4, core: 2. Of those that a mesh axis runs over, the one named last changes fastest.
Arguments:
- atm_state: float32 [2, 72, 256, 2048], P(None, None, 'atm', 'ocn'), may hold values from -6 to 6
- ocn_state: float32 [4, 4, 512, 2048], P(None, None, 'atm', 'ocn'), may hold values from -6 to 6
- land: int32 [512, 2048], P('atm', 'ocn'), may hold values 0 or 1
- ocn_kappa: float32 [512, 2048], P('atm', 'ocn'), may hold values from 0.05 to 0.24
- partner: int32 [16, 512, 1], P('ocn', 'atm'), may hold values from 0 to 15; in each aligned block of 64 rows (0 to 63, 64 to 127, ..., all dimensions but the last counted through in order) at most 8 rows name the same one
- partner_row: int32 [16, 512, 1], P('ocn', 'atm'), may hold values from 0 to 31
- remap_up: float32 [512, 2048, 128], P('atm', 'ocn'), may hold values from -0.375 to 0.375
- remap_down: float32 [512, 2048, 128], P('atm', 'ocn'), may hold values from -0.5 to 0.5
- surface_mix: float32 [4, 16], replicated, may hold values from -1.5 to 1.5
- drag: float32 [256, 2048], P('atm', 'ocn'), may hold values from 0.1 to 1
- level_kappa: float32 [72], replicated, may hold values from 0.05 to 0.2
- vertical_mix: float32 [72, 72], replicated, may hold values from -0.2 to 0.8
- depth_gain: float32 [4], replicated, may hold values from 0.5 to 2
Outputs:
- atm_out: float32 [2, 72, 256, 2048], P(None, None, 'atm', 'ocn')
- ocn_out: float32 [4, 4, 512, 2048], P(None, None, 'atm', 'ocn')
The draws below stay inside these ranges and needn't reach their ends.
Inputs may be any that keep to these rules, and one draw needn't show every extreme that they name: `partner`: of the 64 ocean blocks of one device at most 8 have partners on one atmosphere tile, and some device has exactly 8 on one tile.
All inputs are finite; a program needn't handle non-finite values. No bound on the sum of `land` on one device may be relied on, other than what follows from the above.
Results may differ from the reference program's by a relative error of at most 0.00012.
Values sent between devices are 32-bit elements; how exact they have to be, the bound alone decides.
A program may use at most 128 MiB of HBM per device.

```python
import math
import jax
import jax.numpy as jnp
import numpy as np
from jax import lax

LEV = 72
OLEV = 4
BW = 128
CAX = 32
COX = 64
ASTEPS = 6
OSTEPS = 4
NAX = 256
NAY = 2048
NOX = 512
NOY = 2048
CAP = 8
N_OCN = 16


def draw_vertical_mix(key, part):
    key = jax.random.fold_in(key, 7)
    first, second = jax.random.split(key)
    spread = jnp.clip(jax.random.normal(first, (LEV, LEV), jnp.float32) * 0.15, -0.45, 0.45) / math.sqrt(LEV)
    diagonal = jax.random.uniform(second, (LEV,), jnp.float32, 0.45, 0.75)
    identity = jnp.eye(LEV, dtype=jnp.float32)
    return spread * (1.0 - identity) + identity * diagonal[:, None]


def place_ends(entries, key, smallest, high):
    place = [jax.random.randint(jax.random.fold_in(key, axis), (), 0, length) for axis, length in enumerate(entries.shape)]
    main_axis = entries.shape.index(max(entries.shape))
    beside = place[:main_axis] + [(place[main_axis] + 1) % entries.shape[main_axis]] + place[main_axis + 1:]
    return entries.at[tuple(place)].set(smallest).at[tuple(beside)].set(high)


def block_levels(rng, dims, shards, least, largest):
    level, own = 1.0, jax.random.fold_in(rng, 6)
    for position, parts in shards:
        steps = jnp.exp(jax.random.uniform(jax.random.fold_in(own, position), (parts,), jnp.float32, least / len(shards), largest / len(shards)))
        level = level * jnp.repeat(steps, dims[position] // parts).reshape([-1 if axis == position else 1 for axis in range(len(dims))])
    return level


def assign_block(own_key, own, number, rows, number_of, top, bound, lean):
    order = jax.random.permutation(own_key, number_of)
    crowded, usual = shares(number_of, rows * top, bound, lean, True), shares(number_of, rows * top, bound, lean, False)
    places = jnp.arange(number_of)

    def named(sizes, turn):
        used = int((sizes > 0).sum())
        fixed = max(1, used // 4)
        moved = fixed + (places - fixed + turn * (used - fixed)) % max(1, number_of - fixed)
        return jnp.zeros((number_of,), jnp.int32).at[order[jnp.where(places < fixed, places, moved)]].set(jnp.asarray(sizes, jnp.int32))

    sizes = jnp.where(number % 4 == 0, named(crowded, number // 4), named(usual, number - number // 4 - 1))
    mixed = jax.random.permutation(jax.random.fold_in(own, 3), number_of)
    donor, sink = mixed[0:number_of // 2 * 2:2], mixed[1:number_of // 2 * 2:2]
    room = jnp.minimum(sizes[donor] - 1, bound - sizes[sink]) // 2
    room = jnp.where((donor == order[0]) | (sink == order[0]) | (sizes[sink] == 0), 0, jnp.maximum(room, 0))
    moved = jax.random.randint(jax.random.fold_in(own, 4), (number_of // 2,), 0, 1 << 20) % (room + 1)
    sizes = sizes.at[donor].add(-moved).at[sink].add(moved)
    items = jnp.searchsorted(jnp.cumsum(sizes), jnp.arange(rows * top), side="right").astype(jnp.int32)
    listing = items.reshape(top, rows).T
    listing = listing[jax.random.permutation(jax.random.fold_in(own, 1), rows)]
    turn = jax.random.randint(jax.random.fold_in(own, 2), (rows, 1), 0, top)
    return jnp.take_along_axis(listing, (jnp.arange(top)[None, :] + turn) % top, axis=1)


def shares(number_of, total, reach, skew, full):
    weights = [(1 << 20) // math.isqrt(grade ** skew) + 1 for grade in range(1, number_of + 1)]
    largest = reach if full else min(reach, max(-(-total // number_of), total * weights[0] // sum(weights)))
    least = 1 if total - largest >= number_of - 1 else 0
    counts, rest = [largest] + [least] * (number_of - 1), total - largest - least * (number_of - 1)
    while rest > 0:
        movable = [i for i in range(1, number_of) if counts[i] < largest] or [i for i in range(1, number_of) if counts[i] < reach]
        mass, budget = sum([weights[i] for i in movable]), rest
        for i in movable:
            extra = min(reach - counts[i], max(1, budget * weights[i] // mass), rest)
            counts[i] = counts[i] + extra
            rest = rest - extra
    return np.array(counts)


def normal_values(rng, dims, deviation, limit, cuts=(), held_as=jnp.bfloat16):
    gain = block_levels(rng, dims, cuts, -0.22, 0.18) if cuts else 1.0
    drawn = jax.random.normal(rng, dims, jnp.float32) * deviation * gain
    return jnp.minimum(jnp.maximum(drawn, -limit), limit).astype(held_as)


def setup_inputs(seed: int = 0) -> dict:
    splits = jax.random.split(jax.random.key(seed), 14)
    atm_state = normal_values(splits[0], (2, LEV, NAX, NAY), 1.0, 6.0, ((2, 8), (3, 16)), jnp.float32)
    ocn_state = normal_values(splits[1], (4, OLEV, NOX, NOY), 1.0, 6.0, ((2, 8), (3, 16)), jnp.float32)
    land = place_ends((jax.random.randint(splits[2], (NOX, NOY), 0, 10) < 7).astype(jnp.int32), jax.random.fold_in(splits[2], 1), 0, 1)
    ocn_kappa = jnp.clip(0.05 + 0.19 * jax.random.uniform(splits[3], (NOX, NOY), jnp.float32) ** block_levels(splits[3], (NOX, NOY), ((0, 8), (1, 16)), -0.2, 0.2), 0.05, 0.24)
    partner_keys = jax.random.split(jax.random.fold_in(splits[4], 1), N_OCN * NOX // COX)
    partner_turns = jax.random.permutation(jax.random.fold_in(splits[4], 3), N_OCN * NOX // COX)
    partner = jax.vmap(lambda own, number: assign_block(jax.random.fold_in(splits[4], 2), own, number, COX, N_OCN, 1, CAP, 2))(partner_keys, partner_turns).reshape((N_OCN, NOX, 1))
    partner_row = place_ends(jax.random.randint(splits[5], (N_OCN, NOX, 1), 0, CAX), jax.random.fold_in(splits[5], 1), 0, CAX - 1).astype(jnp.int32)
    remap_up = normal_values(splits[6], (NOX, NOY, BW), (BW * COX // CAX) ** -0.5, 0.375, ((0, 8), (1, 16)), jnp.float32)
    remap_down = normal_values(splits[7], (NOX, NOY, BW), BW ** -0.5, 0.5, ((0, 8), (1, 16)), jnp.float32)
    surface_mix = normal_values(splits[8], (4, 4 * OLEV), (4 * OLEV) ** -0.5, 1.5, (), jnp.float32)
    drag = jnp.clip(jnp.exp(math.log(1.0) - 2.3025851 * jax.random.uniform(splits[9], (NAX, NAY), jnp.float32) ** block_levels(splits[9], (NAX, NAY), ((0, 8), (1, 16)), -0.2, 0.2)), 0.1, 1.0)
    level_kappa = jnp.clip(jax.random.uniform(splits[10], (LEV,), jnp.float32, 0.05, 0.2), 0.05, 0.2)
    vertical_mix = draw_vertical_mix(jax.random.fold_in(splits[13], 71), 0)
    depth_gain = jnp.clip(jnp.exp(jax.random.uniform(splits[12], (OLEV,), jnp.float32, math.log(0.5), math.log(2.0))), 0.5, 2.0)
    return dict(atm_state=atm_state, ocn_state=ocn_state, land=land, ocn_kappa=ocn_kappa, partner=partner, partner_row=partner_row, remap_up=remap_up, remap_down=remap_down, surface_mix=surface_mix, drag=drag, level_kappa=level_kappa, vertical_mix=vertical_mix, depth_gain=depth_gain)


highest = lax.Precision.HIGHEST


def moved(array, across, along):
    return array[..., 1 + across: array.shape[-2] - 1 + across, 1 + along: array.shape[-1] - 1 + along]


def air_step(extended, level_rates, vertical_mix):
    center = moved(extended, 0, 0)
    lateral = moved(extended, 1, 0) + moved(extended, -1, 0) + moved(extended, 0, 1) + moved(extended, 0, -1) - 4.0 * center
    mixed = center + level_rates[:, None, None] * lateral
    levels = vertical_mix.shape[0]
    shaped = mixed.reshape(2, levels, mixed.shape[-2], mixed.shape[-1])
    return jnp.einsum("lm,vmxj->vlxj", vertical_mix, shaped, precision=highest).reshape(mixed.shape)


def ocean_step(extended, land_ext, kappa_ext):
    center = moved(extended, 0, 0)
    total = jnp.zeros_like(center)
    for across, along in ((1, 0), (-1, 0), (0, 1), (0, -1)):
        total = total + moved(land_ext, across, along) * (moved(extended, across, along) - center)
    return center + moved(kappa_ext, 0, 0) * moved(land_ext, 0, 0) * total


def pad_edges(array):
    return jnp.pad(array, [(0, 0)] * (array.ndim - 2) + [(1, 1), (1, 1)])


def reference(atm_state, ocn_state, land, ocn_kappa, partner, partner_row, remap_up, remap_down, surface_mix, drag, level_kappa, vertical_mix, depth_gain):
    land_f = land.astype(jnp.float32)
    channels = 4 * OLEV
    coupled = (ocn_state * land_f).reshape(channels, NOX, N_OCN, BW)
    upward = remap_up.reshape(NOX, N_OCN, BW, BW)
    contrib = jnp.einsum("fxoi,xoij->xofj", coupled, upward, precision=highest)
    target = partner[:, :, 0].T
    target_row = (jnp.arange(NOX, dtype=jnp.int32) // COX)[:, None] * CAX + partner_row[:, :, 0].T
    surface = jnp.zeros((NAX, N_OCN, channels, BW), jnp.float32).at[target_row, target].add(contrib)
    mixed_surface = jnp.einsum("kf,xofj->kxoj", surface_mix, surface, precision=highest).reshape(4, NAX, NAY)
    lowest = atm_state[:, LEV - 1]
    flux = drag[None] * (mixed_surface - jnp.concatenate([lowest, lowest], axis=0))
    air = atm_state.at[:, LEV - 1].add(flux[:2]).reshape(2 * LEV, NAX, NAY)
    rates = jnp.concatenate([level_kappa, level_kappa])
    for number in range(ASTEPS):
        air = air_step(pad_edges(air), rates, vertical_mix)
    partner_flux = flux.reshape(4, NAX, N_OCN, BW)[:, target_row, target, :]
    downward = remap_down.reshape(NOX, N_OCN, BW, BW)
    ocean_flux = jnp.einsum("kxoj,xoij->kxoi", partner_flux, downward, precision=highest).reshape(4, NOX, NOY)
    ocean = ocn_state.reshape(channels, NOX, NOY)
    land_pad = pad_edges(land_f)
    kappa_pad = pad_edges(ocn_kappa)
    for number in range(OSTEPS):
        ocean = ocean_step(pad_edges(ocean), land_pad, kappa_pad)
    ocn_out = ocean.reshape(4, OLEV, NOX, NOY) + depth_gain[None, :, None, None] * ocean_flux[:, None] * land_f
    return air.reshape(2, LEV, NAX, NAY), ocn_out
```

```python
import functools

import jax
import jax.numpy as jnp
from jax import lax
from jax.experimental import pallas as pl
from jax.experimental.pallas import tpu as pltpu
from jax.sharding import PartitionSpec as P

f32 = jnp.float32
bf16 = jnp.bfloat16
LEV = 72
ASTEPS = 6
OSTEPS = 4
ROWS = 32
BLK = 64
W = 128
EXT = ROWS + 2 * ASTEPS
PAIRS = EXT // 2


def mm(a, b, dims=((1,), (0,)), precision=None):
    return lax.dot_general(a, b, (dims, ((), ())), precision=precision, preferred_element_type=f32)


def high(x):
    return x.astype(bf16).astype(f32)


def pick(onehot, x):
    left = onehot.astype(bf16)
    hi = high(x)
    rest = x - hi
    mid = high(rest)
    low = rest - mid
    return mm(left, hi.astype(bf16)) + mm(left, mid.astype(bf16)) + mm(left, low.astype(bf16))


def lanes(shape):
    return lax.broadcasted_iota(jnp.int32, shape, len(shape) - 1)


def rows_of(shape):
    return lax.broadcasted_iota(jnp.int32, shape, len(shape) - 2)


def rolled(x, shift, axis=1):
    if isinstance(shift, int):
        shift = shift % x.shape[axis]
        if shift == 0:
            return x
    return pltpu.roll(x, shift, axis)


def kernel(
    na, no, cap,
    atm, atm_flat, ocn, land, kappa, partner, prow, up, down, smix, drag, lk, vm, gain,
    atm_out, ocn_out,
    a_flat, a_top, a_bot, top_flat, bot_flat, u_own, up_v, down_v,
    r_out, l_out, d_out, l_in, r_in, d_in,
    ob, oe, ob_top, ob_bot, oe_l, oe_r, oe_c,
    rid_out, rid_in, c_out, c_in, p_out, p_in,
    fx, fx_l, fx_r, fx_t, fx_b, fx_c,
    mx, cb, w_s, wf_s, gs, out_a, out_o, us, st,
    p0, p1, p2, p3, p4, p5, p6,
    s0, s1, s2, s3, s4, s5, s6,
    loc, hs, hr, ps, pr,
):
    me_a = lax.axis_index("atm")
    me_o = lax.axis_index("ocn")
    above, below = lax.rem(me_a + na - 1, na), lax.rem(me_a + 1, na)
    left, right = lax.rem(me_o + no - 1, no), lax.rem(me_o + 1, no)
    slots = no * cap
    pm = (p0, p1, p2, p3, p4, p5, p6)
    sm = (s0, s1, s2, s3, s4, s5, s6)

    def local(src, dst, i):
        c = pltpu.make_async_copy(src, dst, loc.at[i])
        c.start()
        return c

    g_ocn = local(ocn, u_own, 0)
    chunks = 4
    part = BLK // chunks
    g_up = [local(up.at[pl.ds(i * part, part)], up_v.at[pl.ds(i * part, part)], 1 + i) for i in range(chunks)]
    g_atm = local(atm_flat, a_flat, 5)
    g_down = local(down, down_v, 6)

    barrier = pltpu.get_barrier_semaphore()
    greeted = [(me_a, lax.rem(me_o + d, no)) for d in range(1, no)]
    greeted += [(r, c) for r in (above, below) for c in (me_o, left, right)]
    for r, c in greeted:
        pl.semaphore_signal(barrier, inc=1, device_id={"atm": r, "ocn": c}, device_id_type=pl.DeviceIdType.MESH)
    pl.semaphore_wait(barrier, len(greeted))

    sent = []

    def send(src, dst, i, r, c):
        d = pltpu.make_async_remote_copy(
            src_ref=src, dst_ref=dst, send_sem=hs.at[i], recv_sem=hr.at[i],
            device_id={"atm": r, "ocn": c}, device_id_type=pl.DeviceIdType.MESH,
        )
        d.start()
        sent.append(d)
        return d

    def spread(src, dst, group):
        made = []
        for d in range(1, no):
            peer = lax.rem(me_o + d, no)
            c = pltpu.make_async_remote_copy(
                src_ref=src.at[pl.ds(pl.multiple_of(peer * cap, 8), cap)],
                dst_ref=dst.at[pl.ds(pl.multiple_of(me_o * cap, 8), cap)],
                send_sem=ps.at[group, d], recv_sem=pr.at[group, d],
                device_id={"atm": me_a, "ocn": peer}, device_id_type=pl.DeviceIdType.MESH,
            )
            c.start()
            sent.append(c)
            made.append(c)
        return made

    def arrive(made):
        for c in made:
            c.wait_recv()

    mine_rows = pl.ds(pl.multiple_of(me_o * cap, 8), cap)

    h_bot = send(atm.at[:, pl.ds(0, 8)], a_bot, 0, above, me_o)
    h_top = send(atm.at[:, pl.ds(ROWS - 8, 8)], a_top, 1, below, me_o)

    t_row = partner[...].astype(f32)
    r_row = prow[...].astype(f32)
    ii, jj = rows_of((BLK, BLK)), lanes((BLK, BLK))
    t_all = jnp.broadcast_to(t_row, (BLK, BLK))
    t_col = jnp.sum(jnp.where(ii == jj, t_all, 0.0), axis=1, keepdims=True)
    same = t_col == t_all
    pos_row = jnp.sum(jnp.where(same & (ii < jj), 1.0, 0.0), axis=0, keepdims=True)
    pos_col = jnp.sum(jnp.where(same & (jj < ii), 1.0, 0.0), axis=1, keepdims=True)
    slot_row = t_row * cap + pos_row
    slot_col = t_col * cap + pos_col
    chosen = jnp.where(rows_of((slots, BLK)).astype(f32) == slot_row, 1.0, 0.0)
    chosen_t = jnp.where(lanes((BLK, slots)).astype(f32) == slot_col, 1.0, 0.0)
    rid = jnp.sum(chosen * (r_row + 1.0), axis=1, keepdims=True) - 1.0
    rid_out[...] = jnp.broadcast_to(rid, (slots, W))
    g_rid = spread(rid_out, rid_in, 0)

    lf = land[...].astype(f32)
    g_ocn.wait()
    for k in range(4):
        total = smix[k, 0] * u_own[0]
        for c in range(1, 16):
            total = total + smix[k, c] * u_own[c]
        total = total * lf
        hi = high(total)
        mx[pl.ds(k, BLK, stride=8), :] = hi
        mx[pl.ds(4 + k, BLK, stride=8), :] = total - hi

    def remap(b, weights, transposed):
        block = weights[b]
        hi = high(block)
        parts = (hi.astype(bf16), (block - hi).astype(bf16))
        vec = mx[pl.ds(pl.multiple_of(b * 8, 8), 8), :].astype(bf16)
        if transposed:
            res = mm(vec, jnp.concatenate(parts, 0), ((1,), (1,)))
        else:
            res = mm(vec, jnp.concatenate(parts, 1))
        first = res[:, :W]
        cb[pl.ds(pl.multiple_of(b * 8, 8), 8), :] = first + rolled(first, 4, 0) + res[:, W:]

    for i in range(chunks):
        g_up[i].wait()
        lax.fori_loop(i * part, (i + 1) * part, lambda b, _: (remap(b, up_v, False), 0)[1], 0, unroll=4)
    fields = jnp.concatenate([cb[pl.ds(k, BLK, stride=8), :] for k in range(4)], 1)
    c_out[...] = pick(chosen, fields)
    g_c = spread(c_out, c_in, 1)

    for c in range(16):
        ob[c] = u_own[c]
    ob[16] = lf
    ob[17] = kappa[...]
    lane64 = lanes((BLK, W))
    edge = jnp.zeros((BLK, W), f32)
    for c in range(16):
        edge = jnp.where(lane64 // 8 == c, rolled(u_own[c], 8 * c + 4), edge)
    oe[0] = edge
    oe[1] = jnp.where(lane64 // 8 == 0, rolled(lf, 4), rolled(kappa[...], 12))
    h_ob = [
        send(ob.at[:, pl.ds(0, 8)], ob_bot, 2, above, me_o),
        send(ob.at[:, pl.ds(BLK - 8, 8)], ob_top, 3, below, me_o),
        send(oe, oe_r, 4, me_a, left),
        send(oe, oe_l, 5, me_a, right),
        send(oe.at[:, pl.ds(BLK - 8, 8)], oe_c.at[0], 6, below, right),
        send(oe.at[:, pl.ds(BLK - 8, 8)], oe_c.at[1], 7, below, left),
        send(oe.at[:, pl.ds(0, 8)], oe_c.at[2], 8, above, right),
        send(oe.at[:, pl.ds(0, 8)], oe_c.at[3], 9, above, left),
    ]

    g_atm.wait()
    lane = lanes((LEV, W))

    def own_row(v, x):
        return a_flat[pl.ds(v * LEV * ROWS + x, LEV, stride=ROWS), :]

    for half in range(2):
        for v in range(2):
            def gather(i, carry):
                to_r, to_l = carry
                row = own_row(v, half * 16 + i)
                here = lane // 8 == i
                return (
                    jnp.where(here, rolled(row, lax.rem(8 * i + 6, W)), to_r),
                    jnp.where(here, rolled(row, 8 * i), to_l),
                )
            to_r, to_l = lax.fori_loop(0, 16, gather, (jnp.zeros((LEV, W), f32), jnp.zeros((LEV, W), f32)))
            r_out[half, v] = to_r
            l_out[half, v] = to_l
    for n, buf in ((0, r_out), (2, l_out)):
        d_out[n] = jnp.where(lane < 64, buf[0, 0], rolled(buf[0, 1], 64))
        d_out[n + 1] = jnp.where(lane < 64, rolled(buf[1, 0], 64), buf[1, 1])
    h_e = [
        send(r_out, l_in, 10, me_a, right),
        send(l_out, r_in, 11, me_a, left),
        send(d_out.at[1], d_in.at[0], 12, below, right),
        send(d_out.at[3], d_in.at[1], 13, below, left),
        send(d_out.at[0], d_in.at[2], 14, above, right),
        send(d_out.at[2], d_in.at[3], 15, above, left),
    ]

    exact = lax.Precision.HIGHEST
    rate = lk[...]
    zpad = jnp.zeros((LEV, W - LEV), f32)
    ca = jnp.concatenate([vm[...] * (1.0 - 4.0 * rate), zpad], 1)
    cc = jnp.concatenate([vm[...] * rate, zpad], 1)
    lhs = jnp.concatenate([ca, cc], 0)[:, :LEV]
    q = mm(lhs, jnp.concatenate([ca, cc], 1), precision=exact)
    q0, q1, q2 = q[:LEV, :W], q[:LEV, W:] + q[LEV:, :W], q[LEV:, W:]
    t = mm(lhs, jnp.concatenate([q0, q1, q2], 1), precision=exact)
    cubes = (
        t[:LEV, :W],
        t[:LEV, W:2 * W] + t[LEV:, :W],
        t[:LEV, 2 * W:] + t[LEV:, W:2 * W],
        t[LEV:, 2 * W:],
    )
    t = mm(jnp.concatenate(cubes, 0)[:, :LEV], jnp.concatenate(cubes, 1), precision=exact)
    wide = []
    column = jnp.zeros((LEV, W), f32)
    for k in range(7):
        m = None
        for i in range(max(0, k - 3), min(3, k) + 1):
            piece = t[LEV * i:LEV * (i + 1), W * (k - i):W * (k - i + 1)]
            m = piece if m is None else m + piece
        hi = high(m)
        z = jnp.zeros((LEV, W), f32)
        hi2 = jnp.concatenate([hi, z], 1)
        wide.append(hi2 + rolled(hi2, 80) + rolled(jnp.concatenate([m - hi, z], 1), 160))
        column = jnp.where(lane == k, rolled(m, k - (LEV - 1)), column)
    wide.append(jnp.zeros((8, 2 * W), f32))
    w_s[...] = jnp.concatenate(wide, 0)[:, :240].astype(bf16)
    chi = high(column)
    wf = chi + rolled(chi, 8) + rolled(column - chi, 16)
    wf_s[...] = jnp.concatenate([wf, jnp.zeros((8, W), f32)], 0)[:, :32].astype(bf16)

    def powers(x):
        hi = high(x)
        z = jnp.zeros((8, 2 * W), f32)
        h = jnp.concatenate([hi, z], 0).astype(bf16)
        m = jnp.concatenate([x - hi, z], 0).astype(bf16)
        return mm(w_s[...], jnp.concatenate([h, m, h], 0))

    def put_row(r, x):
        res = powers(x)
        for k in range(7):
            pm[k][r] = res[LEV * k:LEV * (k + 1)]

    def own_body(x, _):
        put_row(x + ASTEPS, jnp.concatenate([own_row(0, x), own_row(1, x)], 1))
        return 0

    lax.fori_loop(0, ROWS // 2, own_body, 0, unroll=2)

    rid_in[mine_rows] = rid_out[mine_rows]
    c_in[mine_rows] = c_out[mine_rows]
    arrive(g_rid)
    place_t = jnp.where(rid_in[...] == lanes((slots, W)).astype(f32), 1.0, 0.0)
    place = place_t.T[:ROWS]
    arrive(g_c)
    mixed = pick(place, c_in[...])
    flux = []
    for k in range(4):
        flux.append(drag[...] * (mixed[:, W * k:W * (k + 1)] - a_flat[pl.ds(((k % 2) * LEV + LEV - 1) * ROWS, ROWS), :]))
    p_out[...] = pick(place_t[:, :ROWS], jnp.concatenate(flux, 1))
    g_p = spread(p_out, p_in, 2)
    fx[0] = flux[0]
    fx[1] = flux[1]
    h_f = [
        send(fx, fx_r, 16, me_a, left),
        send(fx, fx_l, 17, me_a, right),
        send(fx.at[:, pl.ds(0, 8)], fx_b, 18, above, me_o),
        send(fx.at[:, pl.ds(ROWS - 8, 8)], fx_t, 19, below, me_o),
        send(fx.at[:, pl.ds(ROWS - 8, 8)], fx_c.at[0], 20, below, right),
        send(fx.at[:, pl.ds(ROWS - 8, 8)], fx_c.at[1], 21, below, left),
        send(fx.at[:, pl.ds(0, 8)], fx_c.at[2], 22, above, right),
        send(fx.at[:, pl.ds(0, 8)], fx_c.at[3], 23, above, left),
    ]

    lax.fori_loop(ROWS // 2, ROWS, own_body, 0, unroll=2)

    h_top.wait_recv()
    h_bot.wait_recv()

    top_flat[...] = jnp.where(me_a > 0, a_top[...], 0.0).reshape(2 * LEV * 8, W)
    bot_flat[...] = jnp.where(me_a < na - 1, a_bot[...], 0.0).reshape(2 * LEV * 8, W)

    def beside_row(flat, v, x):
        return flat[pl.ds(v * LEV * 8 + x, LEV, stride=8), :]

    def beside_body(x, _):
        put_row(x, jnp.concatenate([beside_row(top_flat, 0, x + 2), beside_row(top_flat, 1, x + 2)], 1))
        put_row(x + ROWS + ASTEPS, jnp.concatenate([beside_row(bot_flat, 0, x), beside_row(bot_flat, 1, x)], 1))
        return 0

    lax.fori_loop(0, ASTEPS, beside_body, 0)

    arrive(h_e)

    @pl.when(me_o == 0)
    def _():
        l_in[...] = jnp.zeros_like(l_in)
        d_in[0] = jnp.zeros((LEV, W), f32)
        d_in[2] = jnp.zeros((LEV, W), f32)

    @pl.when(me_o == no - 1)
    def _():
        r_in[...] = jnp.zeros_like(r_in)
        d_in[1] = jnp.zeros((LEV, W), f32)
        d_in[3] = jnp.zeros((LEV, W), f32)

    @pl.when(me_a == 0)
    def _():
        d_in[0] = jnp.zeros((LEV, W), f32)
        d_in[1] = jnp.zeros((LEV, W), f32)

    @pl.when(me_a == na - 1)
    def _():
        d_in[2] = jnp.zeros((LEV, W), f32)
        d_in[3] = jnp.zeros((LEV, W), f32)

    def strip(own0, own1, lefts, rights, place0, place1):
        out = jnp.where(lane < 12, own0, rolled(own0, 64))
        out = jnp.where(lane >= 122, rolled(lefts[0], lax.rem(122 + W - place0, W)), out)
        out = jnp.where((lane >= 64) & (lane < 70), rolled(rights[0], lax.rem(64 + W - place0, W)), out)
        out = jnp.where((lane >= 32) & (lane < 44), rolled(own1, 32), out)
        out = jnp.where((lane >= 84) & (lane < 96), rolled(own1, 96), out)
        out = jnp.where((lane >= 26) & (lane < 32), rolled(lefts[1], lax.rem(26 + W - place1, W)), out)
        return jnp.where((lane >= 96) & (lane < 102), rolled(rights[1], lax.rem(96 + W - place1, W)), out)

    def put_pair(pair, x):
        res = powers(x)
        for k in range(7):
            sm[k][pair + 1] = res[LEV * k:LEV * (k + 1)]

    for half in range(2):
        def strip_body(i, _):
            made = []
            for h in range(2):
                n = 2 * i + h
                x = half * 16 + n
                made.append(strip(
                    own_row(0, x), own_row(1, x),
                    (l_in[half, 0], l_in[half, 1]), (r_in[half, 0], r_in[half, 1]), 8 * n, 8 * n,
                ))
            put_pair(half * 8 + i + ASTEPS // 2, jnp.concatenate(made, 1))
            return 0
        lax.fori_loop(0, 8, strip_body, 0)
    for flat, first, base, corner in ((top_flat, 2, 0, 0), (bot_flat, 0, (ROWS + ASTEPS) // 2, 2)):
        def corner_body(i, _):
            made = []
            for h in range(2):
                x = 2 * i + h + first
                made.append(strip(
                    beside_row(flat, 0, x), beside_row(flat, 1, x),
                    (d_in[corner], d_in[corner]), (d_in[corner + 1], d_in[corner + 1]), 8 * x, 8 * x + 64,
                ))
            put_pair(base + i, jnp.concatenate(made, 1))
            return 0
        lax.fori_loop(0, ASTEPS // 2, corner_body, 0)
    for k in range(7):
        sm[k][0] = jnp.zeros((LEV, 2 * W), f32)
        sm[k][PAIRS + 1] = jnp.zeros((LEV, 2 * W), f32)

    lane1 = lanes((1, W))
    outside_l = ((lane1 >= 122) | ((lane1 >= 26) & (lane1 < 32))) & (me_o == 0)
    outside_r = (((lane1 >= 64) & (lane1 < 70)) | ((lane1 >= 96) & (lane1 < 102))) & (me_o == no - 1)
    inside = jnp.where(outside_l | outside_r, 0.0, 1.0)

    for k in range(ASTEPS - 1, -1, -1):
        src, dst = pm[k + 1], pm[k]
        first = ASTEPS - k
        count = EXT - 2 * first
        group = 4 if count % 4 == 0 else 2

        def main_body(i, _):
            r = first + i * group
            for h in range(2):
                sl = slice(W * h, W * (h + 1))
                near = [src[r - 1 + n, :, sl] for n in range(group + 2)]
                made = []
                for n in range(group):
                    c = near[n + 1]
                    made.append(dst[r + n, :, sl] + ((near[n] + near[n + 2]) + (rolled(c, 1) + rolled(c, W - 1))))
                for n in range(group):
                    dst[r + n, :, sl] = made[n]
            return 0
        lax.fori_loop(0, count // group, main_body, 0)

        ssrc, sdst = sm[k + 1], sm[k]

        def strip_step(i, _):
            q = i + first // 2
            a0, a1 = ssrc[q + 1, :, :W], ssrc[q + 1, :, W:]
            made0 = (ssrc[q, :, W:] + a1) + (rolled(a0, 1) + rolled(a0, W - 1))
            made1 = (ssrc[q + 2, :, :W] + a0) + (rolled(a1, 1) + rolled(a1, W - 1))
            sdst[q + 1, :, :W] = sdst[q + 1, :, :W] + made0 * inside
            sdst[q + 1, :, W:] = sdst[q + 1, :, W:] + made1 * inside
            return 0
        lax.fori_loop(0, PAIRS - 2 * (first // 2), strip_step, 0)

        if k:
            @pl.when(me_a == 0)
            def _():
                for r in range(ASTEPS):
                    dst[r] = jnp.zeros((LEV, 2 * W), f32)
                for r in range(ASTEPS // 2):
                    sdst[r + 1] = jnp.zeros((LEV, 2 * W), f32)

            @pl.when(me_a == na - 1)
            def _():
                for r in range(ASTEPS):
                    dst[ROWS + ASTEPS + r] = jnp.zeros((LEV, 2 * W), f32)
                for r in range(ASTEPS // 2):
                    sdst[(ROWS + ASTEPS) // 2 + r + 1] = jnp.zeros((LEV, 2 * W), f32)

    arrive(h_ob)
    tall = BLK + 16
    rr = rows_of((tall, W))
    row_in = ((rr >= 8) | (me_a > 0)) & ((rr < BLK + 8) | (me_a < na - 1))
    lane_t = lanes((tall, W))

    def tall_of(c):
        return jnp.concatenate([ob_top[c], ob[c], ob_bot[c]], 0)

    def tall_edge(n, side):
        body = oe_l[n] if side == 0 else oe_r[n]
        return jnp.concatenate([oe_c[side, n], body, oe_c[2 + side, n]], 0)

    def neighbours(x):
        return (rolled(x, 1, 0) + rolled(x, tall - 1, 0)) + (rolled(x, 1) + rolled(x, W - 1))

    def stepped(x, c0, c1):
        for _ in range(OSTEPS):
            x = c0 * x + c1 * neighbours(x)
        return x

    sea = jnp.where(row_in, tall_of(16), 0.0)
    kap = tall_of(17)
    c1 = kap * sea
    c0 = sea - c1 * neighbours(sea)

    def edges(own, l_edge, r_edge, at, slot):
        out = jnp.where(lane_t < 32 * slot + 4, rolled(l_edge, 32 * slot - at), rolled(own, 32 * slot + 4))
        out = jnp.where(lane_t >= 32 * slot + 16, rolled(own, 32 * slot + 24), out)
        return jnp.where(lane_t >= 32 * slot + 24, rolled(r_edge, 32 * slot + 20 - at), out)

    in_l = (lane_t >= 4) | (me_o > 0)
    in_r = (lane_t < 24) | (me_o < no - 1)
    used = ((lane_t < 12) | ((lane_t >= 16) & (lane_t < 28))) & in_l & in_r & row_in
    tl, tr = tall_edge(1, 0), tall_edge(1, 1)
    e_sea = jnp.where(used, edges(tall_of(16), tl, tr, 0, 0), 0.0)
    e_kap = jnp.where(used, edges(kap, tl, tr, 8, 0), 0.0)

    def four(x):
        return (x + rolled(x, 32)) + (rolled(x, 64) + rolled(x, 96))

    e_sea, e_kap = four(e_sea), four(e_kap)
    e1 = e_kap * e_sea
    e0 = e_sea - e1 * neighbours(e_sea)
    ul, ur = tall_edge(0, 0), tall_edge(0, 1)
    for g in range(4):
        total = edges(tall_of(4 * g), ul, ur, 32 * g, 0)
        for s in range(1, 4):
            c = 4 * g + s
            total = jnp.where(lane_t >= 32 * s, edges(tall_of(c), ul, ur, 8 * c, s), total)
        st[g] = stepped(e_sea * total, e0, e1)[8:8 + BLK]
    for c in range(16):
        mid = stepped(sea * tall_of(c), c0, c1)[8:8 + BLK]
        e = st[c // 4]
        base = 32 * (c % 4)
        mid = jnp.where(lane64 < 4, rolled(e, -base - 4), mid)
        mid = jnp.where(lane64 >= W - 4, rolled(e, 104 - base), mid)
        us[c] = mid + (1.0 - lf) * u_own[c]

    p_in[mine_rows] = p_out[mine_rows]
    arrive(g_p)
    mine = pick(chosen_t, p_in[...])
    for k in range(4):
        x = mine[:, W * k:W * (k + 1)]
        hi = high(x)
        mx[pl.ds(k, BLK, stride=8), :] = hi
        mx[pl.ds(4 + k, BLK, stride=8), :] = x - hi
    g_down.wait()
    lax.fori_loop(0, BLK, lambda b, _: (remap(b, down_v, True), 0)[1], 0, unroll=4)
    for v in range(4):
        term = cb[pl.ds(v, BLK, stride=8), :] * lf
        for n in range(4):
            out_o[4 * v + n] = us[4 * v + n] + gain[0, n] * term
    g_oo = local(out_o, ocn_out, 0)

    arrive(h_f)
    rows48, lanes384 = rows_of((ROWS + 16, 3 * W)), lanes((ROWS + 16, 3 * W))
    grid_in = ((rows48 >= 8) | (me_a > 0)) & ((rows48 < ROWS + 8) | (me_a < na - 1))
    grid_in = grid_in & ((lanes384 >= W) | (me_o > 0)) & ((lanes384 < 2 * W) | (me_o < no - 1))
    grid_in = jnp.where(grid_in, 1.0, 0.0)
    for v in range(2):
        cur = jnp.concatenate([
            jnp.concatenate([fx_c[0, v], fx_t[v], fx_c[1, v]], 1),
            jnp.concatenate([fx_l[v], fx[v], fx_r[v]], 1),
            jnp.concatenate([fx_c[2, v], fx_b[v], fx_c[3, v]], 1),
        ], 0) * grid_in
        for j in range(8):
            if j == 7:
                gs[v, pl.ds(j, ROWS, stride=8), :] = jnp.zeros((ROWS, W), f32)
                break
            gs[v, pl.ds(j, ROWS, stride=8), :] = cur[8:8 + ROWS, W:2 * W]
            if j < 6:
                cur = grid_in * (
                    (rolled(cur, 1, 0) + rolled(cur, ROWS + 15, 0)) + (rolled(cur, 1) + rolled(cur, 3 * W - 1))
                )

    def final_body(i, _):
        for h in range(2):
            x = 2 * i + h
            at = pl.ds(pl.multiple_of(8 * x, 8), 8)
            g = jnp.concatenate([gs[0, at, :], gs[1, at, :]], 1)
            hi = high(g)
            rhs = jnp.concatenate([hi, g - hi, hi, jnp.zeros((8, 2 * W), f32)], 0).astype(bf16)
            extra = mm(wf_s[...], rhs)[:LEV]
            e = s0[i + ASTEPS // 2 + 1, :, W * h:W * (h + 1)]
            for v in range(2):
                res = p0[x + ASTEPS, :, W * v:W * (v + 1)]
                res = jnp.where(lane < 6, rolled(e, -32 * v), res)
                res = jnp.where(lane >= 122, rolled(e, 64 - 32 * v), res)
                out_a[pl.ds(v * LEV * ROWS + x, LEV, stride=ROWS), :] = res + extra[:, W * v:W * (v + 1)]
        return 0

    lax.fori_loop(0, ROWS // 2, final_body, 0)
    g_ao = local(out_a, atm_out, 5)
    for c in sent:
        c.wait_send()
    g_oo.wait()
    g_ao.wait()


def shards(
    na, no,
    atm_state, ocn_state, land, ocn_kappa, partner, partner_row, remap_up, remap_down,
    surface_mix, drag, level_kappa, vertical_mix, depth_gain,
):
    cap = max(2, 2 * BLK // no)
    slots = no * cap
    vmem = pl.BlockSpec(memory_space=pltpu.VMEM)
    smem = pl.BlockSpec(memory_space=pltpu.SMEM)
    hbm = pl.BlockSpec(memory_space=pl.ANY)

    def v(*shape, dtype=f32):
        return pltpu.VMEM(shape, dtype)

    scratch = [
        v(2 * LEV * ROWS, W), v(2 * LEV, 8, W), v(2 * LEV, 8, W), v(2 * LEV * 8, W), v(2 * LEV * 8, W), v(16, BLK, W), v(BLK, W, W), v(BLK, W, W),
        v(2, 2, LEV, W), v(2, 2, LEV, W), v(4, LEV, W), v(2, 2, LEV, W), v(2, 2, LEV, W), v(4, LEV, W),
        v(18, BLK, W), v(2, BLK, W), v(18, 8, W), v(18, 8, W), v(2, BLK, W), v(2, BLK, W), v(4, 2, 8, W),
        v(slots, W), v(slots, W), v(slots, 4 * W), v(slots, 4 * W), v(slots, 4 * W), v(slots, 4 * W),
        v(2, ROWS, W), v(2, ROWS, W), v(2, ROWS, W), v(2, 8, W), v(2, 8, W), v(4, 2, 8, W),
        v(BLK * 8, W), v(BLK * 8, W), v(512, 240, dtype=bf16), v(80, 32, dtype=bf16), v(2, ROWS * 8, W),
        v(2 * LEV * ROWS, W), v(16, BLK, W), v(16, BLK, W), v(4, BLK, W),
    ]
    scratch += [v(EXT, LEV, 2 * W) for _ in range(7)]
    scratch += [v(PAIRS + 2, LEV, 2 * W) for _ in range(7)]
    dma = pltpu.SemaphoreType.DMA
    scratch += [dma((7,)), dma((24,)), dma((24,)), dma((3, no)), dma((3, no))]
    air, sea = pl.pallas_call(
        functools.partial(kernel, na, no, cap),
        out_shape=(
            jax.ShapeDtypeStruct((2 * LEV * ROWS, W), f32),
            jax.ShapeDtypeStruct((16, BLK, W), f32),
        ),
        in_specs=[hbm, hbm, hbm, vmem, vmem, vmem, vmem, hbm, hbm, smem, vmem, vmem, vmem, smem],
        out_specs=(hbm, hbm),
        scratch_shapes=scratch,
        compiler_params=pltpu.CompilerParams(
            collective_id=0, has_side_effects=True, vmem_limit_bytes=63 * 1024 * 1024
        ),
    )(
        atm_state.reshape(2 * LEV, ROWS, W),
        atm_state.reshape(2 * LEV * ROWS, W),
        ocn_state.reshape(16, BLK, W),
        land,
        ocn_kappa,
        partner.reshape(1, BLK),
        partner_row.reshape(1, BLK),
        remap_up,
        remap_down,
        surface_mix,
        drag,
        level_kappa.reshape(1, LEV),
        vertical_mix,
        depth_gain.reshape(1, 4),
    )
    return air.reshape(atm_state.shape), sea.reshape(ocn_state.shape)


def solution(mesh):
    placed = (
        P(None, None, "atm", "ocn"),
        P(None, None, "atm", "ocn"),
        P("atm", "ocn"),
        P("atm", "ocn"),
        P("ocn", "atm", None),
        P("ocn", "atm", None),
        P("atm", "ocn", None),
        P("atm", "ocn", None),
        P(),
        P("atm", "ocn"),
        P(),
        P(),
        P(),
    )
    return jax.shard_map(
        functools.partial(shards, mesh.shape["atm"], mesh.shape["ocn"]),
        mesh=mesh,
        in_specs=placed,
        out_specs=(P(None, None, "atm", "ocn"), P(None, None, "atm", "ocn")),
        check_vma=False,
    )
```

```python
import functools

import jax
import jax.numpy as jnp
import numpy as np
from jax import lax
from jax.experimental import pallas as pl
from jax.experimental.pallas import tpu as pltpu
from jax.sharding import PartitionSpec as P

f32 = jnp.float32
bf16 = jnp.bfloat16
LEV = 72
ASTEPS = 6
OSTEPS = 4
ROWS = 32
BLK = 64
W = 128
EXT = ROWS + 2 * ASTEPS
PAIRS = EXT // 2


def mm(a, b, dims=((1,), (0,)), precision=None):
    return lax.dot_general(a, b, (dims, ((), ())), precision=precision, preferred_element_type=f32)


def high(x):
    return x.astype(bf16).astype(f32)


def pick(onehot, x):
    left = onehot.astype(bf16)
    hi = high(x)
    rest = x - hi
    mid = high(rest)
    low = rest - mid
    return mm(left, hi.astype(bf16)) + mm(left, mid.astype(bf16)) + mm(left, low.astype(bf16))


def lanes(shape):
    return lax.broadcasted_iota(jnp.int32, shape, len(shape) - 1)


def rows_of(shape):
    return lax.broadcasted_iota(jnp.int32, shape, len(shape) - 2)


def rolled(x, shift, axis=1):
    if isinstance(shift, int):
        shift = shift % x.shape[axis]
        if shift == 0:
            return x
    return pltpu.roll(x, shift, axis)


SEG = 3 * ASTEPS
OWN = 2 * ASTEPS


def sines(n):
    k = np.arange(1, n + 1)
    return np.sqrt(2.0 / (n + 1)) * np.sin(np.pi * np.outer(k, k) / (n + 1)), 2.0 * np.cos(np.pi * k / (n + 1))


def two_parts(m):
    hi = np.asarray(m, np.float32).astype(jnp.bfloat16)
    mid = (np.asarray(m, np.float64) - hi.astype(np.float64)).astype(np.float32).astype(jnp.bfloat16)
    return hi, mid


def wide_parts(m):
    hi, mid = two_parts(m)
    return np.concatenate([np.concatenate([hi, mid], 1), np.concatenate([hi, np.zeros_like(mid)], 1)], 0)


def transforms():
    q, d = sines(W)
    back = q.copy()
    back[:, :ASTEPS] = 0.0
    back[:, W - ASTEPS:] = 0.0
    gf, gi, ds = [], [], []
    for kind in range(3):
        there, again, eig = np.zeros((W, W)), np.zeros((W, 2 * W)), np.zeros((1, W))
        for seg in range(4):
            var, side = divmod(seg, 2)
            places = list(range(SEG))
            if kind == 1 and side == 0:
                places = places[ASTEPS:]
            if kind == 2 and side == 1:
                places = places[:OWN]
            basis, values = sines(len(places))
            for n, place in enumerate(places):
                col = place - ASTEPS if side == 0 else W - OWN + place
                if col < 0:
                    lane = 64 + 24 * var + col + ASTEPS
                elif col >= W:
                    lane = 70 + 24 * var + col - W
                else:
                    lane = (col + 24 * var) % W
                there[lane, SEG * seg:SEG * seg + len(places)] = basis[n]
                if ASTEPS <= place < OWN:
                    again[SEG * seg:SEG * seg + len(places), W * var + col] = basis[:, n]
            eig[0, SEG * seg:SEG * seg + len(places)] = values
        gf.append(wide_parts(there))
        hi, mid = two_parts(again)
        gi.append(np.concatenate([hi, hi, mid], 0))
        ds.append(np.concatenate([d.reshape(1, W), eig] + [np.zeros((1, W))] * 6, 0))
    return wide_parts(q), wide_parts(back), np.stack(gf), np.stack(gi), np.stack(ds).astype(np.float32)


def kernel(
    na, no, cap,
    atm, atm_flat, ocn, land, kappa, partner, prow, up, down, smix, drag, lk, vm, gain, qf, qi, gf, gi, eig,
    atm_out, ocn_out,
    a_flat, a_top, a_bot, top_flat, bot_flat, u_own, up_v, down_v,
    own_e, e_out, l_in, r_in, d_in,
    ob, oe, ob_top, ob_bot, oe_l, oe_r, oe_c,
    rid_out, rid_in, c_out, c_in, p_out, p_in,
    fx, fx_l, fx_r, fx_t, fx_b, fx_c,
    mx, cb, w_s, wf_s, gs, out_a, out_o, us, st,
    p0, p1, p2, p3, p4, p5, p6,
    s0, s1, s2, s3, s4, s5, s6,
    loc, hs, hr, ps, pr,
):
    me_a = lax.axis_index("atm")
    me_o = lax.axis_index("ocn")
    above, below = lax.rem(me_a + na - 1, na), lax.rem(me_a + 1, na)
    left, right = lax.rem(me_o + no - 1, no), lax.rem(me_o + 1, no)
    slots = no * cap
    pm = (p0, p1, p2, p3, p4, p5, p6)
    sm = (s0, s1, s2, s3, s4, s5, s6)

    def local(src, dst, i):
        c = pltpu.make_async_copy(src, dst, loc.at[i])
        c.start()
        return c

    g_ocn = local(ocn, u_own, 0)
    chunks = 4
    part = BLK // chunks
    g_up = [local(up.at[pl.ds(i * part, part)], up_v.at[pl.ds(i * part, part)], 1 + i) for i in range(chunks)]
    g_atm = local(atm_flat, a_flat, 5)
    g_down = local(down, down_v, 6)

    barrier = pltpu.get_barrier_semaphore()
    greeted = [(me_a, lax.rem(me_o + d, no)) for d in range(1, no)]
    greeted += [(r, c) for r in (above, below) for c in (me_o, left, right)]
    for r, c in greeted:
        pl.semaphore_signal(barrier, inc=1, device_id={"atm": r, "ocn": c}, device_id_type=pl.DeviceIdType.MESH)
    pl.semaphore_wait(barrier, len(greeted))

    sent = []

    def send(src, dst, i, r, c):
        d = pltpu.make_async_remote_copy(
            src_ref=src, dst_ref=dst, send_sem=hs.at[i], recv_sem=hr.at[i],
            device_id={"atm": r, "ocn": c}, device_id_type=pl.DeviceIdType.MESH,
        )
        d.start()
        sent.append(d)
        return d

    def spread(src, dst, group):
        made = []
        for d in range(1, no):
            peer = lax.rem(me_o + d, no)
            c = pltpu.make_async_remote_copy(
                src_ref=src.at[pl.ds(pl.multiple_of(peer * cap, 8), cap)],
                dst_ref=dst.at[pl.ds(pl.multiple_of(me_o * cap, 8), cap)],
                send_sem=ps.at[group, d], recv_sem=pr.at[group, d],
                device_id={"atm": me_a, "ocn": peer}, device_id_type=pl.DeviceIdType.MESH,
            )
            c.start()
            sent.append(c)
            made.append(c)
        return made

    def arrive(made):
        for c in made:
            c.wait_recv()

    mine_rows = pl.ds(pl.multiple_of(me_o * cap, 8), cap)

    h_bot = send(atm.at[:, pl.ds(0, 8)], a_bot, 0, above, me_o)
    h_top = send(atm.at[:, pl.ds(ROWS - 8, 8)], a_top, 1, below, me_o)

    t_row = partner[...].astype(f32)
    r_row = prow[...].astype(f32)
    ii, jj = rows_of((BLK, BLK)), lanes((BLK, BLK))
    t_all = jnp.broadcast_to(t_row, (BLK, BLK))
    t_col = jnp.sum(jnp.where(ii == jj, t_all, 0.0), axis=1, keepdims=True)
    same = t_col == t_all
    pos_row = jnp.sum(jnp.where(same & (ii < jj), 1.0, 0.0), axis=0, keepdims=True)
    pos_col = jnp.sum(jnp.where(same & (jj < ii), 1.0, 0.0), axis=1, keepdims=True)
    slot_row = t_row * cap + pos_row
    slot_col = t_col * cap + pos_col
    chosen = jnp.where(rows_of((slots, BLK)).astype(f32) == slot_row, 1.0, 0.0)
    chosen_t = jnp.where(lanes((BLK, slots)).astype(f32) == slot_col, 1.0, 0.0)
    rid = jnp.sum(chosen * (r_row + 1.0), axis=1, keepdims=True) - 1.0
    rid_out[...] = jnp.broadcast_to(rid, (slots, W))
    g_rid = spread(rid_out, rid_in, 0)

    lf = land[...].astype(f32)
    g_ocn.wait()
    for k in range(4):
        total = smix[k, 0] * u_own[0]
        for c in range(1, 16):
            total = total + smix[k, c] * u_own[c]
        total = total * lf
        hi = high(total)
        mx[pl.ds(k, BLK, stride=8), :] = hi
        mx[pl.ds(4 + k, BLK, stride=8), :] = total - hi

    def remap(b, weights, transposed):
        block = weights[b]
        hi = high(block)
        parts = (hi.astype(bf16), (block - hi).astype(bf16))
        vec = mx[pl.ds(pl.multiple_of(b * 8, 8), 8), :].astype(bf16)
        if transposed:
            res = mm(vec, jnp.concatenate(parts, 0), ((1,), (1,)))
        else:
            res = mm(vec, jnp.concatenate(parts, 1))
        first = res[:, :W]
        cb[pl.ds(pl.multiple_of(b * 8, 8), 8), :] = first + rolled(first, 4, 0) + res[:, W:]

    for i in range(chunks):
        g_up[i].wait()
        lax.fori_loop(i * part, (i + 1) * part, lambda b, _: (remap(b, up_v, False), 0)[1], 0, unroll=4)
    fields = jnp.concatenate([cb[pl.ds(k, BLK, stride=8), :] for k in range(4)], 1)
    c_out[...] = pick(chosen, fields)
    g_c = spread(c_out, c_in, 1)

    for c in range(16):
        ob[c] = u_own[c]
    ob[16] = lf
    ob[17] = kappa[...]
    lane64 = lanes((BLK, W))
    edge = jnp.zeros((BLK, W), f32)
    for c in range(16):
        edge = jnp.where(lane64 // 8 == c, rolled(u_own[c], 8 * c + 4), edge)
    oe[0] = edge
    oe[1] = jnp.where(lane64 // 8 == 0, rolled(lf, 4), rolled(kappa[...], 12))
    h_ob = [
        send(ob.at[:, pl.ds(0, 8)], ob_bot, 2, above, me_o),
        send(ob.at[:, pl.ds(BLK - 8, 8)], ob_top, 3, below, me_o),
        send(oe, oe_r, 4, me_a, left),
        send(oe, oe_l, 5, me_a, right),
        send(oe.at[:, pl.ds(BLK - 8, 8)], oe_c.at[0], 6, below, right),
        send(oe.at[:, pl.ds(BLK - 8, 8)], oe_c.at[1], 7, below, left),
        send(oe.at[:, pl.ds(0, 8)], oe_c.at[2], 8, above, right),
        send(oe.at[:, pl.ds(0, 8)], oe_c.at[3], 9, above, left),
    ]

    g_atm.wait()
    lane = lanes((LEV, W))

    def own_row(v, x):
        return a_flat[pl.ds(v * LEV * ROWS + x, LEV, stride=ROWS), :]

    def gather(g, xs):
        packed = jnp.zeros((LEV, W), f32)
        for n, x in enumerate(xs):
            if x is not None:
                e = jnp.where((lane >= OWN) & (lane < 3 * OWN), rolled(own_row(1, x), 2 * OWN), own_row(0, x))
                own_e[x] = e
                packed = jnp.where((lane >= 42 * n) & (lane < 42 * n + 42), rolled(e, 42 * n + 6), packed)
        e_out[g] = packed

    lax.fori_loop(0, 5, lambda g, _: (gather(g, [3 * g + n for n in range(3)]), 0)[1], 0)
    gather(5, [15, None, 16])
    lax.fori_loop(6, 11, lambda g, _: (gather(g, [3 * g + n - 1 for n in range(3)]), 0)[1], 0)
    h_e = [
        send(e_out, l_in, 10, me_a, right),
        send(e_out, r_in, 11, me_a, left),
        send(e_out.at[pl.ds(9, 2)], d_in.at[0], 12, below, right),
        send(e_out.at[pl.ds(9, 2)], d_in.at[1], 13, below, left),
        send(e_out.at[pl.ds(0, 2)], d_in.at[2], 14, above, right),
        send(e_out.at[pl.ds(0, 2)], d_in.at[3], 15, above, left),
    ]

    exact = lax.Precision.HIGHEST
    rate = lk[...]
    zpad = jnp.zeros((LEV, W - LEV), f32)
    ca = jnp.concatenate([vm[...] * (1.0 - 4.0 * rate), zpad], 1)
    cc = jnp.concatenate([vm[...] * rate, zpad], 1)
    lhs = jnp.concatenate([ca, cc], 0)[:, :LEV]
    q = mm(lhs, jnp.concatenate([ca, cc], 1), precision=exact)
    q0, q1, q2 = q[:LEV, :W], q[:LEV, W:] + q[LEV:, :W], q[LEV:, W:]
    t = mm(lhs, jnp.concatenate([q0, q1, q2], 1), precision=exact)
    cubes = (
        t[:LEV, :W],
        t[:LEV, W:2 * W] + t[LEV:, :W],
        t[:LEV, 2 * W:] + t[LEV:, W:2 * W],
        t[LEV:, 2 * W:],
    )
    t = mm(jnp.concatenate(cubes, 0)[:, :LEV], jnp.concatenate(cubes, 1), precision=exact)
    wide = []
    column = jnp.zeros((LEV, W), f32)
    for k in range(7):
        m = None
        for i in range(max(0, k - 3), min(3, k) + 1):
            piece = t[LEV * i:LEV * (i + 1), W * (k - i):W * (k - i + 1)]
            m = piece if m is None else m + piece
        hi = high(m)
        z = jnp.zeros((LEV, W), f32)
        hi2 = jnp.concatenate([hi, z], 1)
        wide.append(hi2 + rolled(hi2, 80) + rolled(jnp.concatenate([m - hi, z], 1), 160))
        column = jnp.where(lane == k, rolled(m, k - (LEV - 1)), column)
    wide.append(jnp.zeros((8, 2 * W), f32))
    w_s[...] = jnp.concatenate(wide, 0)[:, :240].astype(bf16)
    chi = high(column)
    wf = chi + rolled(chi, 8) + rolled(column - chi, 16)
    wf_s[...] = jnp.concatenate([wf, jnp.zeros((8, W), f32)], 0)[:, :32].astype(bf16)

    def parts2(x):
        hi = x.astype(bf16)
        return hi, (x - hi.astype(f32)).astype(bf16)

    def changed(rows, matrix):
        res = mm(jnp.concatenate(parts2(jnp.concatenate(rows, 0)), 1), matrix)
        res = res[:, :W] + res[:, W:]
        return [res[LEV * n:LEV * (n + 1)] for n in range(len(rows))]

    def powers(x, low=0):
        hi = high(x)
        z = jnp.zeros((8, 2 * W), f32)
        h = jnp.concatenate([hi, z], 0).astype(bf16)
        m = jnp.concatenate([x - hi, z], 0).astype(bf16)
        return mm(w_s[pl.ds(LEV * low, 512 - LEV * low), :], jnp.concatenate([h, m, h], 0))

    def put(refs, places, rows, matrix, low=0):
        turned = changed(rows, matrix)
        for n, place in enumerate(places):
            res = powers(jnp.concatenate(turned[2 * n:2 * n + 2], 1), low)
            for k in range(low, 7):
                refs[k][place] = res[LEV * (k - low):LEV * (k - low + 1)]

    def own_body(i, _):
        xs = [4 * i + n for n in range(4)]
        put(pm, [x + ASTEPS for x in xs], [own_row(v, x) for x in xs for v in range(2)], qf[...])
        return 0

    lax.fori_loop(0, ROWS // 8, own_body, 0)

    rid_in[mine_rows] = rid_out[mine_rows]
    c_in[mine_rows] = c_out[mine_rows]
    arrive(g_rid)
    place_t = jnp.where(rid_in[...] == lanes((slots, W)).astype(f32), 1.0, 0.0)
    place = place_t.T[:ROWS]
    arrive(g_c)
    mixed = pick(place, c_in[...])
    flux = []
    for k in range(4):
        flux.append(drag[...] * (mixed[:, W * k:W * (k + 1)] - a_flat[pl.ds(((k % 2) * LEV + LEV - 1) * ROWS, ROWS), :]))
    p_out[...] = pick(place_t[:, :ROWS], jnp.concatenate(flux, 1))
    g_p = spread(p_out, p_in, 2)
    fx[0] = flux[0]
    fx[1] = flux[1]
    h_f = [
        send(fx, fx_r, 16, me_a, left),
        send(fx, fx_l, 17, me_a, right),
        send(fx.at[:, pl.ds(0, 8)], fx_b, 18, above, me_o),
        send(fx.at[:, pl.ds(ROWS - 8, 8)], fx_t, 19, below, me_o),
        send(fx.at[:, pl.ds(ROWS - 8, 8)], fx_c.at[0], 20, below, right),
        send(fx.at[:, pl.ds(ROWS - 8, 8)], fx_c.at[1], 21, below, left),
        send(fx.at[:, pl.ds(0, 8)], fx_c.at[2], 22, above, right),
        send(fx.at[:, pl.ds(0, 8)], fx_c.at[3], 23, above, left),
    ]

    lax.fori_loop(ROWS // 8, ROWS // 4, own_body, 0)

    h_top.wait_recv()
    h_bot.wait_recv()

    top_flat[...] = jnp.where(me_a > 0, a_top[...], 0.0).reshape(2 * LEV * 8, W)
    bot_flat[...] = jnp.where(me_a < na - 1, a_bot[...], 0.0).reshape(2 * LEV * 8, W)

    def beside_row(flat, v, x):
        return flat[pl.ds(v * LEV * 8 + x, LEV, stride=8), :]

    for r in range(ASTEPS):
        put(
            pm, [r, EXT - 1 - r],
            [beside_row(top_flat, v, r + 2) for v in range(2)]
            + [beside_row(bot_flat, v, ASTEPS - 1 - r) for v in range(2)],
            qf[...], (ASTEPS - r) // 2 * 2,
        )

    arrive(h_e)
    kind = jnp.where(me_o == 0, 1, jnp.where(me_o == no - 1, 2, 0))
    spot = lax.rem(lane, 42)
    from_left = (spot < 6) | ((spot >= 24) & (spot < 30))

    def strip(e, lefts, rights, n):
        shift = 64 - 42 * n if isinstance(n, int) else lax.rem(64 + W - 42 * n, W)
        beside = rolled(jnp.where(from_left, lefts, rights), shift)
        return jnp.where((lane >= 64) & (lane < 106), beside, e)

    def strip_body(i, _):
        made = []
        for h in range(4):
            x = 4 * i + h
            at = x + jnp.where(i >= 4, 1, 0)
            g = lax.div(at, 3)
            made.append(strip(own_e[x], l_in[g], r_in[g], at - 3 * g))
        put(sm, [2 * i + ASTEPS // 2 + 1, 2 * i + ASTEPS // 2 + 2], made, gf[kind])
        return 0

    lax.fori_loop(0, ROWS // 4, strip_body, 0)
    for q in range(ASTEPS // 2):
        made = []
        for flat, first, corner, there in ((top_flat, 2, 0, me_a > 0), (bot_flat, 0, 2, me_a < na - 1)):
            for h in range(2):
                r = 2 * q + h if corner == 0 else ASTEPS - 2 - 2 * q + h
                e0, e1 = beside_row(flat, 0, r + first), beside_row(flat, 1, r + first)
                e = jnp.where((lane >= OWN) & (lane < 3 * OWN), rolled(e1, 2 * OWN), e0)
                z = strip(e, d_in[corner, r // 3], d_in[corner + 1, r // 3], r % 3)
                made.append(jnp.where(there, z, 0.0))
        put(sm, [q + 1, PAIRS - q], made, gf[kind], (ASTEPS - 2 * q - 1) // 2 * 2)
    s6[0] = jnp.zeros((LEV, 2 * W), f32)
    s6[PAIRS + 1] = jnp.zeros((LEV, 2 * W), f32)

    d_main = jnp.broadcast_to(eig[0, pl.ds(0, 1), :], (LEV, W))
    d_strip = jnp.broadcast_to(eig[kind, pl.ds(1, 1), :], (LEV, W))

    for k in range(ASTEPS - 1, -1, -1):
        src, dst = pm[k + 1], pm[k]
        first = ASTEPS - k
        count = EXT - 2 * first
        group = 4 if count % 4 == 0 else 2

        def main_body(i, _):
            r = first + i * group
            for h in range(2):
                sl = slice(W * h, W * (h + 1))
                near = [src[r - 1 + n, :, sl] for n in range(group + 2)]
                made = []
                for n in range(group):
                    c = near[n + 1]
                    made.append(dst[r + n, :, sl] + ((near[n] + near[n + 2]) + d_main * c))
                for n in range(group):
                    dst[r + n, :, sl] = made[n]
            return 0
        lax.fori_loop(0, count // group, main_body, 0)

        ssrc, sdst = sm[k + 1], sm[k]

        def strip_step(i, _):
            q = i + first // 2
            a0, a1 = ssrc[q + 1, :, :W], ssrc[q + 1, :, W:]
            sdst[q + 1, :, :W] = sdst[q + 1, :, :W] + ((ssrc[q, :, W:] + a1) + d_strip * a0)
            sdst[q + 1, :, W:] = sdst[q + 1, :, W:] + ((ssrc[q + 2, :, :W] + a0) + d_strip * a1)
            return 0
        lax.fori_loop(0, PAIRS - 2 * (first // 2), strip_step, 0)

        if k:
            @pl.when(me_a == 0)
            def _():
                for r in range(ASTEPS):
                    dst[r] = jnp.zeros((LEV, 2 * W), f32)
                for r in range(ASTEPS // 2):
                    sdst[r + 1] = jnp.zeros((LEV, 2 * W), f32)

            @pl.when(me_a == na - 1)
            def _():
                for r in range(ASTEPS):
                    dst[ROWS + ASTEPS + r] = jnp.zeros((LEV, 2 * W), f32)
                for r in range(ASTEPS // 2):
                    sdst[(ROWS + ASTEPS) // 2 + r + 1] = jnp.zeros((LEV, 2 * W), f32)

    arrive(h_ob)
    tall = BLK + 16
    rr = rows_of((tall, W))
    row_in = ((rr >= 8) | (me_a > 0)) & ((rr < BLK + 8) | (me_a < na - 1))
    lane_t = lanes((tall, W))

    def tall_of(c):
        return jnp.concatenate([ob_top[c], ob[c], ob_bot[c]], 0)

    def tall_edge(n, side):
        body = oe_l[n] if side == 0 else oe_r[n]
        return jnp.concatenate([oe_c[side, n], body, oe_c[2 + side, n]], 0)

    def neighbours(x):
        return (rolled(x, 1, 0) + rolled(x, tall - 1, 0)) + (rolled(x, 1) + rolled(x, W - 1))

    def stepped(x, c0, c1):
        for _ in range(OSTEPS):
            x = c0 * x + c1 * neighbours(x)
        return x

    sea = jnp.where(row_in, tall_of(16), 0.0)
    kap = tall_of(17)
    c1 = kap * sea
    c0 = sea - c1 * neighbours(sea)

    def edges(own, l_edge, r_edge, at, slot):
        out = jnp.where(lane_t < 32 * slot + 4, rolled(l_edge, 32 * slot - at), rolled(own, 32 * slot + 4))
        out = jnp.where(lane_t >= 32 * slot + 16, rolled(own, 32 * slot + 24), out)
        return jnp.where(lane_t >= 32 * slot + 24, rolled(r_edge, 32 * slot + 20 - at), out)

    in_l = (lane_t >= 4) | (me_o > 0)
    in_r = (lane_t < 24) | (me_o < no - 1)
    used = ((lane_t < 12) | ((lane_t >= 16) & (lane_t < 28))) & in_l & in_r & row_in
    tl, tr = tall_edge(1, 0), tall_edge(1, 1)
    e_sea = jnp.where(used, edges(tall_of(16), tl, tr, 0, 0), 0.0)
    e_kap = jnp.where(used, edges(kap, tl, tr, 8, 0), 0.0)

    def four(x):
        return (x + rolled(x, 32)) + (rolled(x, 64) + rolled(x, 96))

    e_sea, e_kap = four(e_sea), four(e_kap)
    e1 = e_kap * e_sea
    e0 = e_sea - e1 * neighbours(e_sea)
    ul, ur = tall_edge(0, 0), tall_edge(0, 1)
    for g in range(4):
        total = edges(tall_of(4 * g), ul, ur, 32 * g, 0)
        for s in range(1, 4):
            c = 4 * g + s
            total = jnp.where(lane_t >= 32 * s, edges(tall_of(c), ul, ur, 8 * c, s), total)
        st[g] = stepped(e_sea * total, e0, e1)[8:8 + BLK]
    for c in range(16):
        mid = stepped(sea * tall_of(c), c0, c1)[8:8 + BLK]
        e = st[c // 4]
        base = 32 * (c % 4)
        mid = jnp.where(lane64 < 4, rolled(e, -base - 4), mid)
        mid = jnp.where(lane64 >= W - 4, rolled(e, 104 - base), mid)
        us[c] = mid + (1.0 - lf) * u_own[c]

    p_in[mine_rows] = p_out[mine_rows]
    arrive(g_p)
    mine = pick(chosen_t, p_in[...])
    for k in range(4):
        x = mine[:, W * k:W * (k + 1)]
        hi = high(x)
        mx[pl.ds(k, BLK, stride=8), :] = hi
        mx[pl.ds(4 + k, BLK, stride=8), :] = x - hi
    g_down.wait()
    lax.fori_loop(0, BLK, lambda b, _: (remap(b, down_v, True), 0)[1], 0, unroll=4)
    for v in range(4):
        term = cb[pl.ds(v, BLK, stride=8), :] * lf
        for n in range(4):
            out_o[4 * v + n] = us[4 * v + n] + gain[0, n] * term
    g_oo = local(out_o, ocn_out, 0)

    arrive(h_f)
    rows48, lanes384 = rows_of((ROWS + 16, 3 * W)), lanes((ROWS + 16, 3 * W))
    grid_in = ((rows48 >= 8) | (me_a > 0)) & ((rows48 < ROWS + 8) | (me_a < na - 1))
    grid_in = grid_in & ((lanes384 >= W) | (me_o > 0)) & ((lanes384 < 2 * W) | (me_o < no - 1))
    grid_in = jnp.where(grid_in, 1.0, 0.0)
    for v in range(2):
        cur = jnp.concatenate([
            jnp.concatenate([fx_c[0, v], fx_t[v], fx_c[1, v]], 1),
            jnp.concatenate([fx_l[v], fx[v], fx_r[v]], 1),
            jnp.concatenate([fx_c[2, v], fx_b[v], fx_c[3, v]], 1),
        ], 0) * grid_in
        for j in range(8):
            if j == 7:
                gs[v, pl.ds(j, ROWS, stride=8), :] = jnp.zeros((ROWS, W), f32)
                break
            gs[v, pl.ds(j, ROWS, stride=8), :] = cur[8:8 + ROWS, W:2 * W]
            if j < 6:
                cur = grid_in * (
                    (rolled(cur, 1, 0) + rolled(cur, ROWS + 15, 0)) + (rolled(cur, 1) + rolled(cur, 3 * W - 1))
                )

    def final_body(i, _):
        mids = [p0[2 * i + h + ASTEPS, :, W * v:W * (v + 1)] for h in range(2) for v in range(2)]
        mids = changed(mids, qi[...])
        e = s0[i + ASTEPS // 2 + 1]
        hi, mid = parts2(jnp.concatenate([e[:, :W], e[:, W:]], 0))
        side = mm(jnp.concatenate([hi, mid, hi], 1), gi[kind])
        for h in range(2):
            x = 2 * i + h
            at = pl.ds(pl.multiple_of(8 * x, 8), 8)
            g = jnp.concatenate([gs[0, at, :], gs[1, at, :]], 1)
            hi = high(g)
            rhs = jnp.concatenate([hi, g - hi, hi, jnp.zeros((8, 2 * W), f32)], 0).astype(bf16)
            extra = mm(wf_s[...], rhs)[:LEV] + side[LEV * h:LEV * (h + 1)]
            for v in range(2):
                out_a[pl.ds(v * LEV * ROWS + x, LEV, stride=ROWS), :] = mids[2 * h + v] + extra[:, W * v:W * (v + 1)]
        return 0

    lax.fori_loop(0, ROWS // 2, final_body, 0)
    g_ao = local(out_a, atm_out, 5)
    for c in sent:
        c.wait_send()
    g_oo.wait()
    g_ao.wait()


def shards(
    na, no,
    atm_state, ocn_state, land, ocn_kappa, partner, partner_row, remap_up, remap_down,
    surface_mix, drag, level_kappa, vertical_mix, depth_gain,
):
    cap = max(2, 2 * BLK // no)
    slots = no * cap
    vmem = pl.BlockSpec(memory_space=pltpu.VMEM)
    smem = pl.BlockSpec(memory_space=pltpu.SMEM)
    hbm = pl.BlockSpec(memory_space=pl.ANY)

    def v(*shape, dtype=f32):
        return pltpu.VMEM(shape, dtype)

    scratch = [
        v(2 * LEV * ROWS, W), v(2 * LEV, 8, W), v(2 * LEV, 8, W), v(2 * LEV * 8, W), v(2 * LEV * 8, W), v(16, BLK, W), v(BLK, W, W), v(BLK, W, W),
        v(ROWS, LEV, W), v(11, LEV, W), v(11, LEV, W), v(11, LEV, W), v(4, 2, LEV, W),
        v(18, BLK, W), v(2, BLK, W), v(18, 8, W), v(18, 8, W), v(2, BLK, W), v(2, BLK, W), v(4, 2, 8, W),
        v(slots, W), v(slots, W), v(slots, 4 * W), v(slots, 4 * W), v(slots, 4 * W), v(slots, 4 * W),
        v(2, ROWS, W), v(2, ROWS, W), v(2, ROWS, W), v(2, 8, W), v(2, 8, W), v(4, 2, 8, W),
        v(BLK * 8, W), v(BLK * 8, W), v(512, 240, dtype=bf16), v(80, 32, dtype=bf16), v(2, ROWS * 8, W),
        v(2 * LEV * ROWS, W), v(16, BLK, W), v(16, BLK, W), v(4, BLK, W),
    ]
    scratch += [v(EXT, LEV, 2 * W) for _ in range(7)]
    scratch += [v(PAIRS + 2, LEV, 2 * W) for _ in range(7)]
    dma = pltpu.SemaphoreType.DMA
    scratch += [dma((7,)), dma((24,)), dma((24,)), dma((3, no)), dma((3, no))]
    air, sea = pl.pallas_call(
        functools.partial(kernel, na, no, cap),
        out_shape=(
            jax.ShapeDtypeStruct((2 * LEV * ROWS, W), f32),
            jax.ShapeDtypeStruct((16, BLK, W), f32),
        ),
        in_specs=[hbm, hbm, hbm, vmem, vmem, vmem, vmem, hbm, hbm, smem, vmem, vmem, vmem, smem] + [vmem] * 5,
        out_specs=(hbm, hbm),
        scratch_shapes=scratch,
        compiler_params=pltpu.CompilerParams(
            collective_id=0, has_side_effects=True, vmem_limit_bytes=63 * 1024 * 1024
        ),
    )(
        atm_state.reshape(2 * LEV, ROWS, W),
        atm_state.reshape(2 * LEV * ROWS, W),
        ocn_state.reshape(16, BLK, W),
        land,
        ocn_kappa,
        partner.reshape(1, BLK),
        partner_row.reshape(1, BLK),
        remap_up,
        remap_down,
        surface_mix,
        drag,
        level_kappa.reshape(1, LEV),
        vertical_mix,
        depth_gain.reshape(1, 4),
        *[jnp.asarray(m) for m in transforms()],
    )
    return air.reshape(atm_state.shape), sea.reshape(ocn_state.shape)


def solution(mesh):
    placed = (
        P(None, None, "atm", "ocn"),
        P(None, None, "atm", "ocn"),
        P("atm", "ocn"),
        P("atm", "ocn"),
        P("ocn", "atm", None),
        P("ocn", "atm", None),
        P("atm", "ocn", None),
        P("atm", "ocn", None),
        P(),
        P("atm", "ocn"),
        P(),
        P(),
        P(),
    )
    return jax.shard_map(
        functools.partial(shards, mesh.shape["atm"], mesh.shape["ocn"]),
        mesh=mesh,
        in_specs=placed,
        out_specs=(P(None, None, "atm", "ocn"), P(None, None, "atm", "ocn")),
        check_vma=False,
    )
```

```python
import functools

import jax
import jax.numpy as jnp
import numpy as np
from jax import lax
from jax.experimental import pallas as pl
from jax.experimental.pallas import tpu as pltpu
from jax.sharding import PartitionSpec as P

f32 = jnp.float32
bf16 = jnp.bfloat16
LEV = 72
ASTEPS = 6
OSTEPS = 4
ROWS = 32
BLK = 64
W = 128
EXT = ROWS + 2 * ASTEPS
PAIRS = EXT // 2


def mm(a, b, dims=((1,), (0,)), precision=None):
    return lax.dot_general(a, b, (dims, ((), ())), precision=precision, preferred_element_type=f32)


def high(x):
    return x.astype(bf16).astype(f32)


def pick(onehot, x):
    left = onehot.astype(bf16)
    hi = high(x)
    rest = x - hi
    mid = high(rest)
    low = rest - mid
    return mm(left, hi.astype(bf16)) + mm(left, mid.astype(bf16)) + mm(left, low.astype(bf16))


def lanes(shape):
    return lax.broadcasted_iota(jnp.int32, shape, len(shape) - 1)


def rows_of(shape):
    return lax.broadcasted_iota(jnp.int32, shape, len(shape) - 2)


def rolled(x, shift, axis=1):
    if isinstance(shift, int):
        shift = shift % x.shape[axis]
        if shift == 0:
            return x
    return pltpu.roll(x, shift, axis)


SEG = 3 * ASTEPS
OWN = 2 * ASTEPS


def sines(n):
    k = np.arange(1, n + 1)
    return np.sqrt(2.0 / (n + 1)) * np.sin(np.pi * np.outer(k, k) / (n + 1)), 2.0 * np.cos(np.pi * k / (n + 1))


def two_parts(m):
    hi = np.asarray(m, np.float32).astype(jnp.bfloat16)
    mid = (np.asarray(m, np.float64) - hi.astype(np.float64)).astype(np.float32).astype(jnp.bfloat16)
    return hi, mid


def wide_parts(m):
    hi, mid = two_parts(m)
    return np.concatenate([np.concatenate([hi, mid], 1), np.concatenate([hi, np.zeros_like(mid)], 1)], 0)


def transforms():
    q, d = sines(W)
    back = q.copy()
    back[:, :ASTEPS] = 0.0
    back[:, W - ASTEPS:] = 0.0
    gf, gi, ds = [], [], []
    for kind in range(3):
        there, again, eig = np.zeros((W, W)), np.zeros((W, 2 * W)), np.zeros((1, W))
        for seg in range(4):
            var, side = divmod(seg, 2)
            places = list(range(SEG))
            if kind == 1 and side == 0:
                places = places[ASTEPS:]
            if kind == 2 and side == 1:
                places = places[:OWN]
            basis, values = sines(len(places))
            for n, place in enumerate(places):
                col = place - ASTEPS if side == 0 else W - OWN + place
                if col < 0:
                    lane = 64 + 24 * var + col + ASTEPS
                elif col >= W:
                    lane = 70 + 24 * var + col - W
                else:
                    lane = (col + 24 * var) % W
                there[lane, SEG * seg:SEG * seg + len(places)] = basis[n]
                if ASTEPS <= place < OWN:
                    again[SEG * seg:SEG * seg + len(places), W * var + col] = basis[:, n]
            eig[0, SEG * seg:SEG * seg + len(places)] = values
        gf.append(wide_parts(there))
        hi, mid = two_parts(again)
        gi.append(np.concatenate([hi, hi, mid], 0))
        ds.append(np.concatenate([d.reshape(1, W), eig] + [np.zeros((1, W))] * 6, 0))
    return wide_parts(q), wide_parts(back), np.stack(gf), np.stack(gi), np.stack(ds).astype(np.float32)


def kernel(
    na, no, cap,
    atm, atm_flat, ocn, land, kappa, partner, prow, up, down, smix, drag, lk, vm, gain, qf, qi, gf, gi, eig,
    atm_out, ocn_out,
    a_flat, a_top, a_bot, top_flat, bot_flat, u_own, up_v, down_v,
    own_e, r_out, l_out, l_in, r_in, d_in,
    ob, oe, ob_top, ob_bot, oe_l, oe_r, oe_c,
    rid_out, rid_in, c_out, c_in, p_out, p_in,
    fx, fx_l, fx_r, fx_t, fx_b, fx_c,
    mx, cb, w_s, wf_s, gs, out_a, out_o, us, st,
    p0, p1, p2, p3, p4, p5, p6,
    s0, s1, s2, s3, s4, s5, s6,
    loc, hs, hr, ps, pr,
):
    me_a = lax.axis_index("atm")
    me_o = lax.axis_index("ocn")
    above, below = lax.rem(me_a + na - 1, na), lax.rem(me_a + 1, na)
    left, right = lax.rem(me_o + no - 1, no), lax.rem(me_o + 1, no)
    slots = no * cap
    pm = (p0, p1, p2, p3, p4, p5, p6)
    sm = (s0, s1, s2, s3, s4, s5, s6)

    def local(src, dst, i):
        c = pltpu.make_async_copy(src, dst, loc.at[i])
        c.start()
        return c

    g_ocn = local(ocn, u_own, 0)
    chunks = 4
    part = BLK // chunks
    g_up = [local(up.at[pl.ds(i * part, part)], up_v.at[pl.ds(i * part, part)], 1 + i) for i in range(chunks)]
    g_atm = local(atm_flat, a_flat, 5)
    g_down = local(down, down_v, 6)

    barrier = pltpu.get_barrier_semaphore()
    greeted = [(me_a, lax.rem(me_o + d, no)) for d in range(1, no)]
    greeted += [(r, c) for r in (above, below) for c in (me_o, left, right)]
    for r, c in greeted:
        pl.semaphore_signal(barrier, inc=1, device_id={"atm": r, "ocn": c}, device_id_type=pl.DeviceIdType.MESH)
    pl.semaphore_wait(barrier, len(greeted))

    sent = []

    def send(src, dst, i, r, c):
        d = pltpu.make_async_remote_copy(
            src_ref=src, dst_ref=dst, send_sem=hs.at[i], recv_sem=hr.at[i],
            device_id={"atm": r, "ocn": c}, device_id_type=pl.DeviceIdType.MESH,
        )
        d.start()
        sent.append(d)
        return d

    def spread(src, dst, group):
        made = []
        for d in range(1, no):
            peer = lax.rem(me_o + d, no)
            c = pltpu.make_async_remote_copy(
                src_ref=src.at[pl.ds(pl.multiple_of(peer * cap, 8), cap)],
                dst_ref=dst.at[pl.ds(pl.multiple_of(me_o * cap, 8), cap)],
                send_sem=ps.at[group, d], recv_sem=pr.at[group, d],
                device_id={"atm": me_a, "ocn": peer}, device_id_type=pl.DeviceIdType.MESH,
            )
            c.start()
            sent.append(c)
            made.append(c)
        return made

    def arrive(made):
        for c in made:
            c.wait_recv()

    mine_rows = pl.ds(pl.multiple_of(me_o * cap, 8), cap)

    lf = land[...].astype(f32)
    g_ocn.wait()
    for c in range(16):
        ob[c] = u_own[c]
    ob[16] = lf
    ob[17] = kappa[...]
    lane64 = lanes((BLK, W))
    edge = jnp.zeros((BLK, W), f32)
    for c in range(16):
        edge = jnp.where(lane64 // 8 == c, rolled(u_own[c], 8 * c + 4), edge)
    oe[0] = edge
    oe[1] = jnp.where(lane64 // 8 == 0, rolled(lf, 4), rolled(kappa[...], 12))
    h_ob = [
        send(ob.at[:, pl.ds(0, 8)], ob_bot, 2, above, me_o),
        send(ob.at[:, pl.ds(BLK - 8, 8)], ob_top, 3, below, me_o),
        send(oe, oe_r, 4, me_a, left),
        send(oe, oe_l, 5, me_a, right),
        send(oe.at[:, pl.ds(BLK - 8, 8)], oe_c.at[0], 6, below, right),
        send(oe.at[:, pl.ds(BLK - 8, 8)], oe_c.at[1], 7, below, left),
        send(oe.at[:, pl.ds(0, 8)], oe_c.at[2], 8, above, right),
        send(oe.at[:, pl.ds(0, 8)], oe_c.at[3], 9, above, left),
    ]

    h_bot = send(atm.at[:, pl.ds(0, 8)], a_bot, 0, above, me_o)
    h_top = send(atm.at[:, pl.ds(ROWS - 8, 8)], a_top, 1, below, me_o)

    t_row = partner[...].astype(f32)
    r_row = prow[...].astype(f32)
    ii, jj = rows_of((BLK, BLK)), lanes((BLK, BLK))
    t_all = jnp.broadcast_to(t_row, (BLK, BLK))
    t_col = jnp.sum(jnp.where(ii == jj, t_all, 0.0), axis=1, keepdims=True)
    same = t_col == t_all
    pos_row = jnp.sum(jnp.where(same & (ii < jj), 1.0, 0.0), axis=0, keepdims=True)
    pos_col = jnp.sum(jnp.where(same & (jj < ii), 1.0, 0.0), axis=1, keepdims=True)
    slot_row = t_row * cap + pos_row
    slot_col = t_col * cap + pos_col
    chosen = jnp.where(rows_of((slots, BLK)).astype(f32) == slot_row, 1.0, 0.0)
    chosen_t = jnp.where(lanes((BLK, slots)).astype(f32) == slot_col, 1.0, 0.0)
    rid = jnp.sum(chosen * (r_row + 1.0), axis=1, keepdims=True) - 1.0
    rid_out[...] = jnp.broadcast_to(rid, (slots, W))
    g_rid = spread(rid_out, rid_in, 0)

    for k in range(4):
        total = smix[k, 0] * u_own[0]
        for c in range(1, 16):
            total = total + smix[k, c] * u_own[c]
        total = total * lf
        hi = high(total)
        mx[pl.ds(k, BLK, stride=8), :] = hi
        mx[pl.ds(4 + k, BLK, stride=8), :] = total - hi

    def remap(b, weights, transposed):
        block = weights[b]
        hi = high(block)
        parts = (hi.astype(bf16), (block - hi).astype(bf16))
        vec = mx[pl.ds(pl.multiple_of(b * 8, 8), 8), :].astype(bf16)
        if transposed:
            res = mm(vec, jnp.concatenate(parts, 0), ((1,), (1,)))
        else:
            res = mm(vec, jnp.concatenate(parts, 1))
        first = res[:, :W]
        cb[pl.ds(pl.multiple_of(b * 8, 8), 8), :] = first + rolled(first, 4, 0) + res[:, W:]

    for i in range(chunks):
        g_up[i].wait()
        lax.fori_loop(i * part, (i + 1) * part, lambda b, _: (remap(b, up_v, False), 0)[1], 0, unroll=4)
    fields = jnp.concatenate([cb[pl.ds(k, BLK, stride=8), :] for k in range(4)], 1)
    c_out[...] = pick(chosen, fields)
    g_c = spread(c_out, c_in, 1)

    g_atm.wait()
    lane = lanes((LEV, W))

    def own_row(v, x):
        return a_flat[pl.ds(v * LEV * ROWS + x, LEV, stride=ROWS), :]

    def gather(g, _):
        to_r = to_l = jnp.zeros((LEV, W), f32)
        for n in range(8):
            x = 8 * g + n
            e = jnp.where((lane >= OWN) & (lane < 3 * OWN), rolled(own_row(1, x), 2 * OWN), own_row(0, x))
            own_e[x] = e
            place = 6 * (n % 4) + 48 * (n // 4)
            here = (lane // 48 == n // 4) & (lax.rem(lane, 24) // 6 == n % 4)
            to_r = jnp.where(here, rolled(e, place + 6), to_r)
            to_l = jnp.where(here, rolled(e, place), to_l)
        r_out[g] = to_r
        l_out[g] = to_l
        return 0

    lax.fori_loop(0, ROWS // 8, gather, 0)
    h_e = [
        send(r_out, l_in, 10, me_a, right),
        send(l_out, r_in, 11, me_a, left),
        send(r_out.at[3], d_in.at[0], 12, below, right),
        send(l_out.at[3], d_in.at[1], 13, below, left),
        send(r_out.at[0], d_in.at[2], 14, above, right),
        send(l_out.at[0], d_in.at[3], 15, above, left),
    ]

    exact = lax.Precision.HIGHEST
    rate = lk[...]
    zpad = jnp.zeros((LEV, W - LEV), f32)
    ca = jnp.concatenate([vm[...] * (1.0 - 4.0 * rate), zpad], 1)
    cc = jnp.concatenate([vm[...] * rate, zpad], 1)
    lhs = jnp.concatenate([ca, cc], 0)[:, :LEV]
    q = mm(lhs, jnp.concatenate([ca, cc], 1), precision=exact)
    q0, q1, q2 = q[:LEV, :W], q[:LEV, W:] + q[LEV:, :W], q[LEV:, W:]
    t = mm(lhs, jnp.concatenate([q0, q1, q2], 1), precision=exact)
    cubes = (
        t[:LEV, :W],
        t[:LEV, W:2 * W] + t[LEV:, :W],
        t[:LEV, 2 * W:] + t[LEV:, W:2 * W],
        t[LEV:, 2 * W:],
    )
    t = mm(jnp.concatenate(cubes, 0)[:, :LEV], jnp.concatenate(cubes, 1), precision=exact)
    wide = []
    column = jnp.zeros((LEV, W), f32)
    for k in range(7):
        m = None
        for i in range(max(0, k - 3), min(3, k) + 1):
            piece = t[LEV * i:LEV * (i + 1), W * (k - i):W * (k - i + 1)]
            m = piece if m is None else m + piece
        hi = high(m)
        z = jnp.zeros((LEV, W), f32)
        hi2 = jnp.concatenate([hi, z], 1)
        wide.append(hi2 + rolled(hi2, 80) + rolled(jnp.concatenate([m - hi, z], 1), 160))
        column = jnp.where(lane == k, rolled(m, k - (LEV - 1)), column)
    wide.append(jnp.zeros((8, 2 * W), f32))
    w_s[...] = jnp.concatenate(wide, 0)[:, :240].astype(bf16)
    chi = high(column)
    wf = chi + rolled(chi, 8) + rolled(column - chi, 16)
    wf_s[...] = jnp.concatenate([wf, jnp.zeros((8, W), f32)], 0)[:, :32].astype(bf16)

    def parts2(x):
        hi = x.astype(bf16)
        return hi, (x - hi.astype(f32)).astype(bf16)

    def changed(rows, matrix):
        res = mm(jnp.concatenate(parts2(jnp.concatenate(rows, 0)), 1), matrix)
        res = res[:, :W] + res[:, W:]
        return [res[LEV * n:LEV * (n + 1)] for n in range(len(rows))]

    def powers(x, low=0):
        hi = high(x)
        z = jnp.zeros((8, 2 * W), f32)
        h = jnp.concatenate([hi, z], 0).astype(bf16)
        m = jnp.concatenate([x - hi, z], 0).astype(bf16)
        return mm(w_s[pl.ds(LEV * low, 512 - LEV * low), :], jnp.concatenate([h, m, h], 0))

    def put(refs, places, rows, matrix, low=0):
        turned = changed(rows, matrix)
        for n, place in enumerate(places):
            res = powers(jnp.concatenate(turned[2 * n:2 * n + 2], 1), low)
            for k in range(low, 7):
                refs[k][place] = res[LEV * (k - low):LEV * (k - low + 1)]

    arrive(h_ob)
    tall = BLK + 16
    rr = rows_of((tall, W))
    row_in = ((rr >= 8) | (me_a > 0)) & ((rr < BLK + 8) | (me_a < na - 1))
    lane_t = lanes((tall, W))

    def tall_of(c):
        return jnp.concatenate([ob_top[c], ob[c], ob_bot[c]], 0)

    def tall_edge(n, side):
        body = oe_l[n] if side == 0 else oe_r[n]
        return jnp.concatenate([oe_c[side, n], body, oe_c[2 + side, n]], 0)

    def neighbours(x):
        return (rolled(x, 1, 0) + rolled(x, tall - 1, 0)) + (rolled(x, 1) + rolled(x, W - 1))

    def stepped(x, c0, c1):
        for _ in range(OSTEPS):
            x = c0 * x + c1 * neighbours(x)
        return x

    sea = jnp.where(row_in, tall_of(16), 0.0)
    kap = tall_of(17)
    c1 = kap * sea
    c0 = sea - c1 * neighbours(sea)

    def edges(own, l_edge, r_edge, at, slot):
        out = jnp.where(lane_t < 32 * slot + 4, rolled(l_edge, 32 * slot - at), rolled(own, 32 * slot + 4))
        out = jnp.where(lane_t >= 32 * slot + 16, rolled(own, 32 * slot + 24), out)
        return jnp.where(lane_t >= 32 * slot + 24, rolled(r_edge, 32 * slot + 20 - at), out)

    in_l = (lane_t >= 4) | (me_o > 0)
    in_r = (lane_t < 24) | (me_o < no - 1)
    used = ((lane_t < 12) | ((lane_t >= 16) & (lane_t < 28))) & in_l & in_r & row_in
    tl, tr = tall_edge(1, 0), tall_edge(1, 1)
    e_sea = jnp.where(used, edges(tall_of(16), tl, tr, 0, 0), 0.0)
    e_kap = jnp.where(used, edges(kap, tl, tr, 8, 0), 0.0)

    def four(x):
        return (x + rolled(x, 32)) + (rolled(x, 64) + rolled(x, 96))

    e_sea, e_kap = four(e_sea), four(e_kap)
    e1 = e_kap * e_sea
    e0 = e_sea - e1 * neighbours(e_sea)
    ul, ur = tall_edge(0, 0), tall_edge(0, 1)
    for g in range(4):
        total = edges(tall_of(4 * g), ul, ur, 32 * g, 0)
        for s in range(1, 4):
            c = 4 * g + s
            total = jnp.where(lane_t >= 32 * s, edges(tall_of(c), ul, ur, 8 * c, s), total)
        st[g] = stepped(e_sea * total, e0, e1)[8:8 + BLK]

    def channel(c, e, slot):
        mid = stepped(sea * tall_of(c), c0, c1)[8:8 + BLK]
        mid = jnp.where(lane64 < 4, rolled(e, lax.rem(2 * W - 32 * slot - 4, W)), mid)
        mid = jnp.where(lane64 >= W - 4, rolled(e, lax.rem(W + 104 - 32 * slot, W)), mid)
        us[c] = mid + (1.0 - lf) * u_own[c]

    def own_body(i, _):
        xs = [4 * i + n for n in range(4)]
        put(pm, [x + ASTEPS for x in xs], [own_row(v, x) for x in xs for v in range(2)], qf[...])
        for h in range(2):
            slot = 2 * lax.rem(i, 2) + h
            channel(2 * i + h, st[lax.div(i, 2)], slot)
        return 0

    lax.fori_loop(0, ROWS // 4, own_body, 0)

    rid_in[mine_rows] = rid_out[mine_rows]
    c_in[mine_rows] = c_out[mine_rows]
    arrive(g_rid)
    place_t = jnp.where(rid_in[...] == lanes((slots, W)).astype(f32), 1.0, 0.0)
    place = place_t.T[:ROWS]
    arrive(g_c)
    mixed = pick(place, c_in[...])
    flux = []
    for k in range(4):
        flux.append(drag[...] * (mixed[:, W * k:W * (k + 1)] - a_flat[pl.ds(((k % 2) * LEV + LEV - 1) * ROWS, ROWS), :]))
    p_out[...] = pick(place_t[:, :ROWS], jnp.concatenate(flux, 1))
    g_p = spread(p_out, p_in, 2)
    fx[0] = flux[0]
    fx[1] = flux[1]
    h_f = [
        send(fx, fx_r, 16, me_a, left),
        send(fx, fx_l, 17, me_a, right),
        send(fx.at[:, pl.ds(0, 8)], fx_b, 18, above, me_o),
        send(fx.at[:, pl.ds(ROWS - 8, 8)], fx_t, 19, below, me_o),
        send(fx.at[:, pl.ds(ROWS - 8, 8)], fx_c.at[0], 20, below, right),
        send(fx.at[:, pl.ds(ROWS - 8, 8)], fx_c.at[1], 21, below, left),
        send(fx.at[:, pl.ds(0, 8)], fx_c.at[2], 22, above, right),
        send(fx.at[:, pl.ds(0, 8)], fx_c.at[3], 23, above, left),
    ]

    h_top.wait_recv()
    h_bot.wait_recv()

    top_flat[...] = jnp.where(me_a > 0, a_top[...], 0.0).reshape(2 * LEV * 8, W)
    bot_flat[...] = jnp.where(me_a < na - 1, a_bot[...], 0.0).reshape(2 * LEV * 8, W)

    def beside_row(flat, v, x):
        return flat[pl.ds(v * LEV * 8 + x, LEV, stride=8), :]

    for r in range(ASTEPS):
        put(
            pm, [r, EXT - 1 - r],
            [beside_row(top_flat, v, r + 2) for v in range(2)]
            + [beside_row(bot_flat, v, ASTEPS - 1 - r) for v in range(2)],
            qf[...], (ASTEPS - r) // 2 * 2,
        )

    d_main = jnp.broadcast_to(eig[0, pl.ds(0, 1), :], (LEV, W))
    for k in range(ASTEPS - 1, -1, -1):
        src, dst = pm[k + 1], pm[k]
        first = ASTEPS - k
        count = EXT - 2 * first
        group = 4 if count % 4 == 0 else 2

        def main_body(i, _):
            r = first + i * group
            for h in range(2):
                sl = slice(W * h, W * (h + 1))
                near = [src[r - 1 + n, :, sl] for n in range(group + 2)]
                made = []
                for n in range(group):
                    c = near[n + 1]
                    made.append(dst[r + n, :, sl] + ((near[n] + near[n + 2]) + d_main * c))
                for n in range(group):
                    dst[r + n, :, sl] = made[n]
            return 0
        lax.fori_loop(0, count // group, main_body, 0)

        if k:
            @pl.when(me_a == 0)
            def _():
                for r in range(ASTEPS):
                    dst[r] = jnp.zeros((LEV, 2 * W), f32)

            @pl.when(me_a == na - 1)
            def _():
                for r in range(ASTEPS):
                    dst[ROWS + ASTEPS + r] = jnp.zeros((LEV, 2 * W), f32)

    arrive(h_e)
    kind = jnp.where(me_o == 0, 1, jnp.where(me_o == no - 1, 2, 0))
    spot = lax.rem(lane + 8, 24)
    from_left = (lane >= 64) & (lane < 112) & (spot < 6)
    from_right = (lane >= 64) & (lane < 112) & (spot >= 6) & (spot < 12)

    def strip(e, lefts, rights, n):
        place = 6 * (n % 4) + 48 * (n // 4)
        return jnp.where(from_left, rolled(lefts, 64 - place), jnp.where(from_right, rolled(rights, 70 - place), e))

    def strip_body(i, _):
        for n in range(0, 8, 4):
            made = []
            for h in range(n, n + 4):
                made.append(strip(own_e[8 * i + h], l_in[i], r_in[i], h))
            at = 4 * i + n // 2 + ASTEPS // 2 + 1
            put(sm, [at, at + 1], made, gf[kind])
        return 0

    lax.fori_loop(0, ROWS // 8, strip_body, 0)
    for q in range(ASTEPS // 2):
        made = []
        for flat, first, corner, there in ((top_flat, 2, 0, me_a > 0), (bot_flat, 0, 2, me_a < na - 1)):
            for h in range(2):
                r = 2 * q + h if corner == 0 else ASTEPS - 2 - 2 * q + h
                e0, e1 = beside_row(flat, 0, r + first), beside_row(flat, 1, r + first)
                e = jnp.where((lane >= OWN) & (lane < 3 * OWN), rolled(e1, 2 * OWN), e0)
                z = strip(e, d_in[corner], d_in[corner + 1], r + first)
                made.append(jnp.where(there, z, 0.0))
        put(sm, [q + 1, PAIRS - q], made, gf[kind], (ASTEPS - 2 * q - 1) // 2 * 2)
    s6[0] = jnp.zeros((LEV, 2 * W), f32)
    s6[PAIRS + 1] = jnp.zeros((LEV, 2 * W), f32)

    d_strip = jnp.broadcast_to(eig[kind, pl.ds(1, 1), :], (LEV, W))
    for k in range(ASTEPS - 1, -1, -1):
        ssrc, sdst = sm[k + 1], sm[k]
        first = ASTEPS - k

        def strip_step(i, _):
            q = i + first // 2
            a0, a1 = ssrc[q + 1, :, :W], ssrc[q + 1, :, W:]
            sdst[q + 1, :, :W] = sdst[q + 1, :, :W] + ((ssrc[q, :, W:] + a1) + d_strip * a0)
            sdst[q + 1, :, W:] = sdst[q + 1, :, W:] + ((ssrc[q + 2, :, :W] + a0) + d_strip * a1)
            return 0
        lax.fori_loop(0, PAIRS - 2 * (first // 2), strip_step, 0)

        if k:
            @pl.when(me_a == 0)
            def _():
                for r in range(ASTEPS // 2):
                    sdst[r + 1] = jnp.zeros((LEV, 2 * W), f32)

            @pl.when(me_a == na - 1)
            def _():
                for r in range(ASTEPS // 2):
                    sdst[(ROWS + ASTEPS) // 2 + r + 1] = jnp.zeros((LEV, 2 * W), f32)

    p_in[mine_rows] = p_out[mine_rows]
    arrive(g_p)
    mine = pick(chosen_t, p_in[...])
    for k in range(4):
        x = mine[:, W * k:W * (k + 1)]
        hi = high(x)
        mx[pl.ds(k, BLK, stride=8), :] = hi
        mx[pl.ds(4 + k, BLK, stride=8), :] = x - hi
    g_down.wait()
    lax.fori_loop(0, BLK, lambda b, _: (remap(b, down_v, True), 0)[1], 0, unroll=4)
    for v in range(4):
        term = cb[pl.ds(v, BLK, stride=8), :] * lf
        for n in range(4):
            out_o[4 * v + n] = us[4 * v + n] + gain[0, n] * term
    g_oo = local(out_o, ocn_out, 0)

    arrive(h_f)
    rows48, lanes384 = rows_of((ROWS + 16, 3 * W)), lanes((ROWS + 16, 3 * W))
    grid_in = ((rows48 >= 8) | (me_a > 0)) & ((rows48 < ROWS + 8) | (me_a < na - 1))
    grid_in = grid_in & ((lanes384 >= W) | (me_o > 0)) & ((lanes384 < 2 * W) | (me_o < no - 1))
    grid_in = jnp.where(grid_in, 1.0, 0.0)
    for v in range(2):
        cur = jnp.concatenate([
            jnp.concatenate([fx_c[0, v], fx_t[v], fx_c[1, v]], 1),
            jnp.concatenate([fx_l[v], fx[v], fx_r[v]], 1),
            jnp.concatenate([fx_c[2, v], fx_b[v], fx_c[3, v]], 1),
        ], 0) * grid_in
        for j in range(8):
            if j == 7:
                gs[v, pl.ds(j, ROWS, stride=8), :] = jnp.zeros((ROWS, W), f32)
                break
            gs[v, pl.ds(j, ROWS, stride=8), :] = cur[8:8 + ROWS, W:2 * W]
            if j < 6:
                cur = grid_in * (
                    (rolled(cur, 1, 0) + rolled(cur, ROWS + 15, 0)) + (rolled(cur, 1) + rolled(cur, 3 * W - 1))
                )

    def final_body(i, _):
        mids = [p0[2 * i + h + ASTEPS, :, W * v:W * (v + 1)] for h in range(2) for v in range(2)]
        mids = changed(mids, qi[...])
        e = s0[i + ASTEPS // 2 + 1]
        hi, mid = parts2(jnp.concatenate([e[:, :W], e[:, W:]], 0))
        side = mm(jnp.concatenate([hi, mid, hi], 1), gi[kind])
        for h in range(2):
            x = 2 * i + h
            at = pl.ds(pl.multiple_of(8 * x, 8), 8)
            g = jnp.concatenate([gs[0, at, :], gs[1, at, :]], 1)
            hi = high(g)
            rhs = jnp.concatenate([hi, g - hi, hi, jnp.zeros((8, 2 * W), f32)], 0).astype(bf16)
            extra = mm(wf_s[...], rhs)[:LEV] + side[LEV * h:LEV * (h + 1)]
            for v in range(2):
                out_a[pl.ds(v * LEV * ROWS + x, LEV, stride=ROWS), :] = mids[2 * h + v] + extra[:, W * v:W * (v + 1)]
        return 0

    lax.fori_loop(0, ROWS // 2, final_body, 0, unroll=2)
    g_ao = local(out_a, atm_out, 5)
    for c in sent:
        c.wait_send()
    g_oo.wait()
    g_ao.wait()


def shards(
    na, no,
    atm_state, ocn_state, land, ocn_kappa, partner, partner_row, remap_up, remap_down,
    surface_mix, drag, level_kappa, vertical_mix, depth_gain,
):
    cap = max(2, 2 * BLK // no)
    slots = no * cap
    vmem = pl.BlockSpec(memory_space=pltpu.VMEM)
    smem = pl.BlockSpec(memory_space=pltpu.SMEM)
    hbm = pl.BlockSpec(memory_space=pl.ANY)

    def v(*shape, dtype=f32):
        return pltpu.VMEM(shape, dtype)

    scratch = [
        v(2 * LEV * ROWS, W), v(2 * LEV, 8, W), v(2 * LEV, 8, W), v(2 * LEV * 8, W), v(2 * LEV * 8, W), v(16, BLK, W), v(BLK, W, W), v(BLK, W, W),
        v(ROWS, LEV, W), v(4, LEV, W), v(4, LEV, W), v(4, LEV, W), v(4, LEV, W), v(4, LEV, W),
        v(18, BLK, W), v(2, BLK, W), v(18, 8, W), v(18, 8, W), v(2, BLK, W), v(2, BLK, W), v(4, 2, 8, W),
        v(slots, W), v(slots, W), v(slots, 4 * W), v(slots, 4 * W), v(slots, 4 * W), v(slots, 4 * W),
        v(2, ROWS, W), v(2, ROWS, W), v(2, ROWS, W), v(2, 8, W), v(2, 8, W), v(4, 2, 8, W),
        v(BLK * 8, W), v(BLK * 8, W), v(512, 240, dtype=bf16), v(80, 32, dtype=bf16), v(2, ROWS * 8, W),
        v(2 * LEV * ROWS, W), v(16, BLK, W), v(16, BLK, W), v(4, BLK, W),
    ]
    scratch += [v(EXT, LEV, 2 * W) for _ in range(7)]
    scratch += [v(PAIRS + 2, LEV, 2 * W) for _ in range(7)]
    dma = pltpu.SemaphoreType.DMA
    scratch += [dma((7,)), dma((24,)), dma((24,)), dma((3, no)), dma((3, no))]
    air, sea = pl.pallas_call(
        functools.partial(kernel, na, no, cap),
        out_shape=(
            jax.ShapeDtypeStruct((2 * LEV * ROWS, W), f32),
            jax.ShapeDtypeStruct((16, BLK, W), f32),
        ),
        in_specs=[hbm, hbm, hbm, vmem, vmem, vmem, vmem, hbm, hbm, smem, vmem, vmem, vmem, smem] + [vmem] * 5,
        out_specs=(hbm, hbm),
        scratch_shapes=scratch,
        compiler_params=pltpu.CompilerParams(
            collective_id=0, has_side_effects=True, vmem_limit_bytes=63 * 1024 * 1024
        ),
    )(
        atm_state.reshape(2 * LEV, ROWS, W),
        atm_state.reshape(2 * LEV * ROWS, W),
        ocn_state.reshape(16, BLK, W),
        land,
        ocn_kappa,
        partner.reshape(1, BLK),
        partner_row.reshape(1, BLK),
        remap_up,
        remap_down,
        surface_mix,
        drag,
        level_kappa.reshape(1, LEV),
        vertical_mix,
        depth_gain.reshape(1, 4),
        *[jnp.asarray(m) for m in transforms()],
    )
    return air.reshape(atm_state.shape), sea.reshape(ocn_state.shape)


def solution(mesh):
    placed = (
        P(None, None, "atm", "ocn"),
        P(None, None, "atm", "ocn"),
        P("atm", "ocn"),
        P("atm", "ocn"),
        P("ocn", "atm", None),
        P("ocn", "atm", None),
        P("atm", "ocn", None),
        P("atm", "ocn", None),
        P(),
        P("atm", "ocn"),
        P(),
        P(),
        P(),
    )
    return jax.shard_map(
        functools.partial(shards, mesh.shape["atm"], mesh.shape["ocn"]),
        mesh=mesh,
        in_specs=placed,
        out_specs=(P(None, None, "atm", "ocn"), P(None, None, "atm", "ocn")),
        check_vma=False,
    )
```

```python
import functools

import jax
import jax.numpy as jnp
import numpy as np
from jax import lax
from jax.experimental import pallas as pl
from jax.experimental.pallas import tpu as pltpu
from jax.sharding import PartitionSpec as P

f32 = jnp.float32
bf16 = jnp.bfloat16
LEV = 72
ASTEPS = 6
OSTEPS = 4
ROWS = 32
BLK = 64
W = 128
EXT = ROWS + 2 * ASTEPS
PAIRS = EXT // 2


def mm(a, b, dims=((1,), (0,)), precision=None):
    return lax.dot_general(a, b, (dims, ((), ())), precision=precision, preferred_element_type=f32)


def high(x):
    return x.astype(bf16).astype(f32)


def pick(onehot, x):
    left = onehot.astype(bf16)
    hi = high(x)
    rest = x - hi
    mid = high(rest)
    low = rest - mid
    return mm(left, hi.astype(bf16)) + mm(left, mid.astype(bf16)) + mm(left, low.astype(bf16))


def lanes(shape):
    return lax.broadcasted_iota(jnp.int32, shape, len(shape) - 1)


def rows_of(shape):
    return lax.broadcasted_iota(jnp.int32, shape, len(shape) - 2)


def rolled(x, shift, axis=1):
    if isinstance(shift, int):
        shift = shift % x.shape[axis]
        if shift == 0:
            return x
    return pltpu.roll(x, shift, axis)


def parts2(x):
    hi = x.astype(bf16)
    return hi, (x - hi.astype(f32)).astype(bf16)


def changed(rows, matrix):
    res = mm(jnp.concatenate(parts2(jnp.concatenate(rows, 0)), 1), matrix)
    res = res[:, :W] + res[:, W:]
    return [res[LEV * n:LEV * (n + 1)] for n in range(len(rows))]


SEG = 3 * ASTEPS
OWN = 2 * ASTEPS


def sines(n):
    k = np.arange(1, n + 1)
    return np.sqrt(2.0 / (n + 1)) * np.sin(np.pi * np.outer(k, k) / (n + 1)), 2.0 * np.cos(np.pi * k / (n + 1))


def two_parts(m):
    hi = np.asarray(m, np.float32).astype(jnp.bfloat16)
    mid = (np.asarray(m, np.float64) - hi.astype(np.float64)).astype(np.float32).astype(jnp.bfloat16)
    return hi, mid


def wide_parts(m):
    hi, mid = two_parts(m)
    return np.concatenate([np.concatenate([hi, mid], 1), np.concatenate([hi, np.zeros_like(mid)], 1)], 0)


def transforms():
    q, d = sines(W)
    back = q.copy()
    back[:, :ASTEPS] = 0.0
    back[:, W - ASTEPS:] = 0.0
    gf, gi, ds = [], [], []
    for kind in range(3):
        there, again, eig = np.zeros((W, W)), np.zeros((W, 2 * W)), np.zeros((1, W))
        for seg in range(4):
            var, side = divmod(seg, 2)
            places = list(range(SEG))
            if kind == 1 and side == 0:
                places = places[ASTEPS:]
            if kind == 2 and side == 1:
                places = places[:OWN]
            basis, values = sines(len(places))
            for n, place in enumerate(places):
                col = place - ASTEPS if side == 0 else W - OWN + place
                if col < 0:
                    lane = 64 + 24 * var + col + ASTEPS
                elif col >= W:
                    lane = 70 + 24 * var + col - W
                else:
                    lane = (col + 24 * var) % W
                there[lane, SEG * seg:SEG * seg + len(places)] = basis[n]
                if ASTEPS <= place < OWN:
                    again[SEG * seg:SEG * seg + len(places), W * var + col] = basis[:, n]
            eig[0, SEG * seg:SEG * seg + len(places)] = values
        gf.append(wide_parts(there))
        hi, mid = two_parts(again)
        gi.append(np.concatenate([hi, hi, mid], 0))
        ds.append(np.concatenate([d.reshape(1, W), eig] + [np.zeros((1, W))] * 6, 0))
    return wide_parts(q), wide_parts(back), np.stack(gf), np.stack(gi), np.stack(ds).astype(np.float32)


def kernel(
    na, no, cap,
    atm, atm_flat, ocn, land, kappa, partner, prow, up, down, smix, drag, lk, vm, qf_all, gf_all, eig,
    p_res, s_res, g_res, w_res, u_res, t_res,
    a_flat, a_top, a_bot, top_flat, bot_flat, u_own, up_v, down_v,
    own_e, r_out, l_out, l_in, r_in, d_in,
    ob, oe, ob_top, ob_bot, oe_l, oe_r, oe_c,
    rid_out, rid_in, c_out, c_in, p_out, p_in,
    fx, fx_l, fx_r, fx_t, fx_b, fx_c,
    mx, cb, w_s, wf_s, gs, us, st, term, qf, gf,
    p0, p1, p2, p3, p4, p5, p6,
    s0, s1, s2, s3, s4, s5, s6,
    loc, hs, hr, ps, pr,
):
    me_a = lax.axis_index("atm")
    me_o = lax.axis_index("ocn")
    above, below = lax.rem(me_a + na - 1, na), lax.rem(me_a + 1, na)
    left, right = lax.rem(me_o + no - 1, no), lax.rem(me_o + 1, no)
    slots = no * cap
    pm = (p0, p1, p2, p3, p4, p5, p6)
    sm = (s0, s1, s2, s3, s4, s5, s6)

    def local(src, dst, i):
        c = pltpu.make_async_copy(src, dst, loc.at[i])
        c.start()
        return c

    g_ocn = local(ocn, u_own, 0)
    chunks = 4
    part = BLK // chunks
    g_up = [local(up.at[pl.ds(i * part, part)], up_v.at[pl.ds(i * part, part)], 1 + i) for i in range(chunks)]
    g_atm = local(atm_flat, a_flat, 5)
    kind = jnp.where(me_o == 0, 1, jnp.where(me_o == no - 1, 2, 0))
    g_qf = local(qf_all, qf, 7)

    barrier = pltpu.get_barrier_semaphore()
    greeted = [(me_a, lax.rem(me_o + d, no)) for d in range(1, no)]
    greeted += [(r, c) for r in (above, below) for c in (me_o, left, right)]
    for r, c in greeted:
        pl.semaphore_signal(barrier, inc=1, device_id={"atm": r, "ocn": c}, device_id_type=pl.DeviceIdType.MESH)
    pl.semaphore_wait(barrier, len(greeted))

    sent = []
    lane = lanes((LEV, W))

    def send(src, dst, i, r, c):
        d = pltpu.make_async_remote_copy(
            src_ref=src, dst_ref=dst, send_sem=hs.at[i], recv_sem=hr.at[i],
            device_id={"atm": r, "ocn": c}, device_id_type=pl.DeviceIdType.MESH,
        )
        d.start()
        sent.append(d)
        return d

    def spread(src, dst, group):
        made = []
        for d in range(1, no):
            peer = lax.rem(me_o + d, no)
            c = pltpu.make_async_remote_copy(
                src_ref=src.at[pl.ds(pl.multiple_of(peer * cap, 8), cap)],
                dst_ref=dst.at[pl.ds(pl.multiple_of(me_o * cap, 8), cap)],
                send_sem=ps.at[group, d], recv_sem=pr.at[group, d],
                device_id={"atm": me_a, "ocn": peer}, device_id_type=pl.DeviceIdType.MESH,
            )
            c.start()
            sent.append(c)
            made.append(c)
        return made

    def arrive(made):
        for c in made:
            c.wait_recv()

    mine_rows = pl.ds(pl.multiple_of(me_o * cap, 8), cap)

    lf = land[...].astype(f32)
    g_ocn.wait()
    for c in range(16):
        ob[c] = u_own[c]
    ob[16] = lf
    ob[17] = kappa[...]
    lane64 = lanes((BLK, W))
    edge = jnp.zeros((BLK, W), f32)
    for c in range(16):
        edge = jnp.where(lane64 // 8 == c, rolled(u_own[c], 8 * c + 4), edge)
    oe[0] = edge
    oe[1] = jnp.where(lane64 // 8 == 0, rolled(lf, 4), rolled(kappa[...], 12))
    h_ob = [
        send(ob.at[:, pl.ds(0, 8)], ob_bot, 2, above, me_o),
        send(ob.at[:, pl.ds(BLK - 8, 8)], ob_top, 3, below, me_o),
        send(oe, oe_r, 4, me_a, left),
        send(oe, oe_l, 5, me_a, right),
        send(oe.at[:, pl.ds(BLK - 8, 8)], oe_c.at[0], 6, below, right),
        send(oe.at[:, pl.ds(BLK - 8, 8)], oe_c.at[1], 7, below, left),
        send(oe.at[:, pl.ds(0, 8)], oe_c.at[2], 8, above, right),
        send(oe.at[:, pl.ds(0, 8)], oe_c.at[3], 9, above, left),
    ]

    h_bot = send(atm.at[:, pl.ds(0, 8)], a_bot, 0, above, me_o)
    h_top = send(atm.at[:, pl.ds(ROWS - 8, 8)], a_top, 1, below, me_o)

    t_row = partner[...].astype(f32)
    r_row = prow[...].astype(f32)
    ii, jj = rows_of((BLK, BLK)), lanes((BLK, BLK))
    t_all = jnp.broadcast_to(t_row, (BLK, BLK))
    t_col = jnp.sum(jnp.where(ii == jj, t_all, 0.0), axis=1, keepdims=True)
    same = t_col == t_all
    pos_row = jnp.sum(jnp.where(same & (ii < jj), 1.0, 0.0), axis=0, keepdims=True)
    pos_col = jnp.sum(jnp.where(same & (jj < ii), 1.0, 0.0), axis=1, keepdims=True)
    slot_row = t_row * cap + pos_row
    slot_col = t_col * cap + pos_col
    chosen = jnp.where(rows_of((slots, BLK)).astype(f32) == slot_row, 1.0, 0.0)
    chosen_t = jnp.where(lanes((BLK, slots)).astype(f32) == slot_col, 1.0, 0.0)
    rid = jnp.sum(chosen * (r_row + 1.0), axis=1, keepdims=True) - 1.0
    rid_out[...] = jnp.broadcast_to(rid, (slots, W))
    g_rid = spread(rid_out, rid_in, 0)

    exact = lax.Precision.HIGHEST
    rate = lk[...]
    zpad = jnp.zeros((LEV, W - LEV), f32)
    ca = jnp.concatenate([vm[...] * (1.0 - 4.0 * rate), zpad], 1)
    cc = jnp.concatenate([vm[...] * rate, zpad], 1)
    lhs = jnp.concatenate([ca, cc], 0)[:, :LEV]
    q = mm(lhs, jnp.concatenate([ca, cc], 1), precision=exact)
    q0, q1, q2 = q[:LEV, :W], q[:LEV, W:] + q[LEV:, :W], q[LEV:, W:]
    t = mm(lhs, jnp.concatenate([q0, q1, q2], 1), precision=exact)
    cubes = (
        t[:LEV, :W],
        t[:LEV, W:2 * W] + t[LEV:, :W],
        t[:LEV, 2 * W:] + t[LEV:, W:2 * W],
        t[LEV:, 2 * W:],
    )
    t = mm(jnp.concatenate(cubes, 0)[:, :LEV], jnp.concatenate(cubes, 1), precision=exact)
    wide = []
    column = jnp.zeros((LEV, W), f32)
    for k in range(7):
        m = None
        for i in range(max(0, k - 3), min(3, k) + 1):
            piece = t[LEV * i:LEV * (i + 1), W * (k - i):W * (k - i + 1)]
            m = piece if m is None else m + piece
        hi = high(m)
        z = jnp.zeros((LEV, W), f32)
        hi2 = jnp.concatenate([hi, z], 1)
        wide.append(hi2 + rolled(hi2, 80) + rolled(jnp.concatenate([m - hi, z], 1), 160))
        column = jnp.where(lane == k, rolled(m, k - (LEV - 1)), column)
    wide.append(jnp.zeros((8, 2 * W), f32))
    w_s[...] = jnp.concatenate(wide, 0)[:, :240].astype(bf16)
    chi = high(column)
    wf = chi + rolled(chi, 8) + rolled(column - chi, 16)
    wf_s[...] = jnp.concatenate([wf, jnp.zeros((8, W), f32)], 0)[:, :32].astype(bf16)
    done = [local(wf_s, w_res, 9)]

    for k in range(4):
        total = smix[k, 0] * u_own[0]
        for c in range(1, 16):
            total = total + smix[k, c] * u_own[c]
        total = total * lf
        hi = high(total)
        mx[pl.ds(k, BLK, stride=8), :] = hi
        mx[pl.ds(4 + k, BLK, stride=8), :] = total - hi

    def remap(b, weights, transposed):
        block = weights[b]
        hi = high(block)
        parts = (hi.astype(bf16), (block - hi).astype(bf16))
        vec = mx[pl.ds(pl.multiple_of(b * 8, 8), 8), :].astype(bf16)
        if transposed:
            res = mm(vec, jnp.concatenate(parts, 0), ((1,), (1,)))
        else:
            res = mm(vec, jnp.concatenate(parts, 1))
        first = res[:, :W]
        cb[pl.ds(pl.multiple_of(b * 8, 8), 8), :] = first + rolled(first, 4, 0) + res[:, W:]

    def own_row(v, x):
        return a_flat[pl.ds(v * LEV * ROWS + x, LEV, stride=ROWS), :]

    def gather(g, _):
        to_r = to_l = jnp.zeros((LEV, W), f32)
        for n in range(8):
            x = 8 * g + n
            e = jnp.where((lane >= OWN) & (lane < 3 * OWN), rolled(own_row(1, x), 2 * OWN), own_row(0, x))
            own_e[x] = e
            place = 6 * (n % 4) + 48 * (n // 4)
            here = (lane // 48 == n // 4) & (lax.rem(lane, 24) // 6 == n % 4)
            to_r = jnp.where(here, rolled(e, place + 6), to_r)
            to_l = jnp.where(here, rolled(e, place), to_l)
        r_out[g] = to_r
        l_out[g] = to_l

    def gather_remap(g, _):
        for n in range(16):
            remap(16 * g + n, up_v, False)
        gather(g, _)
        return 0

    for i in range(chunks):
        g_up[i].wait()
    g_atm.wait()
    lax.fori_loop(0, 4, gather_remap, 0)
    g_gf = local(gf_all.at[kind], gf, 8)
    g_down = local(down, down_v, 6)
    fields = jnp.concatenate([cb[pl.ds(k, BLK, stride=8), :] for k in range(4)], 1)
    c_out[...] = pick(chosen, fields)
    g_c = spread(c_out, c_in, 1)


    h_e = [
        send(r_out, l_in, 10, me_a, right),
        send(l_out, r_in, 11, me_a, left),
        send(r_out.at[3], d_in.at[0], 12, below, right),
        send(l_out.at[3], d_in.at[1], 13, below, left),
        send(r_out.at[0], d_in.at[2], 14, above, right),
        send(l_out.at[0], d_in.at[3], 15, above, left),
    ]

    def powers(x, low=0):
        hi = high(x)
        z = jnp.zeros((8, 2 * W), f32)
        h = jnp.concatenate([hi, z], 0).astype(bf16)
        m = jnp.concatenate([x - hi, z], 0).astype(bf16)
        return mm(w_s[pl.ds(LEV * low, 512 - LEV * low), :], jnp.concatenate([h, m, h], 0))

    def put(refs, places, rows, matrix, low=0):
        turned = changed(rows, matrix)
        for n, place in enumerate(places):
            res = powers(jnp.concatenate(turned[2 * n:2 * n + 2], 1), low)
            for k in range(low, 7):
                refs[k][place] = res[LEV * (k - low):LEV * (k - low + 1)]

    arrive(h_ob)
    tall = BLK + 16
    rr = rows_of((tall, W))
    row_in = ((rr >= 8) | (me_a > 0)) & ((rr < BLK + 8) | (me_a < na - 1))
    lane_t = lanes((tall, W))

    def tall_of(c):
        return jnp.concatenate([ob_top[c], ob[c], ob_bot[c]], 0)

    def tall_edge(n, side):
        body = oe_l[n] if side == 0 else oe_r[n]
        return jnp.concatenate([oe_c[side, n], body, oe_c[2 + side, n]], 0)

    def neighbours(x):
        return (rolled(x, 1, 0) + rolled(x, tall - 1, 0)) + (rolled(x, 1) + rolled(x, W - 1))

    def stepped(x, c0, c1):
        for _ in range(OSTEPS):
            x = c0 * x + c1 * neighbours(x)
        return x

    sea = jnp.where(row_in, tall_of(16), 0.0)
    kap = tall_of(17)
    c1 = kap * sea
    c0 = sea - c1 * neighbours(sea)

    def edges(own, l_edge, r_edge, at, slot):
        out = jnp.where(lane_t < 32 * slot + 4, rolled(l_edge, 32 * slot - at), rolled(own, 32 * slot + 4))
        out = jnp.where(lane_t >= 32 * slot + 16, rolled(own, 32 * slot + 24), out)
        return jnp.where(lane_t >= 32 * slot + 24, rolled(r_edge, 32 * slot + 20 - at), out)

    in_l = (lane_t >= 4) | (me_o > 0)
    in_r = (lane_t < 24) | (me_o < no - 1)
    used = ((lane_t < 12) | ((lane_t >= 16) & (lane_t < 28))) & in_l & in_r & row_in
    tl, tr = tall_edge(1, 0), tall_edge(1, 1)
    e_sea = jnp.where(used, edges(tall_of(16), tl, tr, 0, 0), 0.0)
    e_kap = jnp.where(used, edges(kap, tl, tr, 8, 0), 0.0)

    def four(x):
        return (x + rolled(x, 32)) + (rolled(x, 64) + rolled(x, 96))

    e_sea, e_kap = four(e_sea), four(e_kap)
    e1 = e_kap * e_sea
    e0 = e_sea - e1 * neighbours(e_sea)
    ul, ur = tall_edge(0, 0), tall_edge(0, 1)
    for g in range(4):
        total = edges(tall_of(4 * g), ul, ur, 32 * g, 0)
        for s in range(1, 4):
            c = 4 * g + s
            total = jnp.where(lane_t >= 32 * s, edges(tall_of(c), ul, ur, 8 * c, s), total)
        st[g] = stepped(e_sea * total, e0, e1)[8:8 + BLK]

    def channel(c, e, slot):
        mid = stepped(sea * tall_of(c), c0, c1)[8:8 + BLK]
        mid = jnp.where(lane64 < 4, rolled(e, lax.rem(2 * W - 32 * slot - 4, W)), mid)
        mid = jnp.where(lane64 >= W - 4, rolled(e, lax.rem(W + 104 - 32 * slot, W)), mid)
        us[c] = mid + (1.0 - lf) * u_own[c]

    g_qf.wait()

    def own_body(i, _):
        xs = [4 * i + n for n in range(4)]
        put(pm, [x + ASTEPS for x in xs], [own_row(v, x) for x in xs for v in range(2)], qf[...])
        for h in range(2):
            slot = 2 * lax.rem(i, 2) + h
            channel(2 * i + h, st[lax.div(i, 2)], slot)
        return 0

    lax.fori_loop(0, ROWS // 4, own_body, 0)

    done.append(local(us, u_res, 10))

    rid_in[mine_rows] = rid_out[mine_rows]
    c_in[mine_rows] = c_out[mine_rows]
    arrive(g_rid)
    place_t = jnp.where(rid_in[...] == lanes((slots, W)).astype(f32), 1.0, 0.0)
    place = place_t.T[:ROWS]
    arrive(g_c)
    mixed = pick(place, c_in[...])
    flux = []
    for k in range(4):
        flux.append(drag[...] * (mixed[:, W * k:W * (k + 1)] - a_flat[pl.ds(((k % 2) * LEV + LEV - 1) * ROWS, ROWS), :]))
    p_out[...] = pick(place_t[:, :ROWS], jnp.concatenate(flux, 1))
    g_p = spread(p_out, p_in, 2)
    fx[0] = flux[0]
    fx[1] = flux[1]
    h_f = [
        send(fx, fx_r, 16, me_a, left),
        send(fx, fx_l, 17, me_a, right),
        send(fx.at[:, pl.ds(0, 8)], fx_b, 18, above, me_o),
        send(fx.at[:, pl.ds(ROWS - 8, 8)], fx_t, 19, below, me_o),
        send(fx.at[:, pl.ds(ROWS - 8, 8)], fx_c.at[0], 20, below, right),
        send(fx.at[:, pl.ds(ROWS - 8, 8)], fx_c.at[1], 21, below, left),
        send(fx.at[:, pl.ds(0, 8)], fx_c.at[2], 22, above, right),
        send(fx.at[:, pl.ds(0, 8)], fx_c.at[3], 23, above, left),
    ]

    h_top.wait_recv()
    h_bot.wait_recv()

    top_flat[...] = jnp.where(me_a > 0, a_top[...], 0.0).reshape(2 * LEV * 8, W)
    bot_flat[...] = jnp.where(me_a < na - 1, a_bot[...], 0.0).reshape(2 * LEV * 8, W)

    def beside_row(flat, v, x):
        return flat[pl.ds(v * LEV * 8 + x, LEV, stride=8), :]

    for r in range(ASTEPS):
        put(
            pm, [r, EXT - 1 - r],
            [beside_row(top_flat, v, r + 2) for v in range(2)]
            + [beside_row(bot_flat, v, ASTEPS - 1 - r) for v in range(2)],
            qf[...], (ASTEPS - r) // 2 * 2,
        )

    d_main = jnp.broadcast_to(eig[0, pl.ds(0, 1), :], (LEV, W))
    for k in range(ASTEPS - 1, -1, -1):
        src, dst = pm[k + 1], pm[k]
        first = ASTEPS - k
        count = EXT - 2 * first
        group = 4 if count % 4 == 0 else 2

        def main_body(i, _):
            r = first + i * group
            for h in range(2):
                sl = slice(W * h, W * (h + 1))
                near = [src[r - 1 + n, :, sl] for n in range(group + 2)]
                made = []
                for n in range(group):
                    c = near[n + 1]
                    made.append(dst[r + n, :, sl] + ((near[n] + near[n + 2]) + d_main * c))
                for n in range(group):
                    dst[r + n, :, sl] = made[n]
            return 0
        lax.fori_loop(0, count // group, main_body, 0)

        if k:
            @pl.when(me_a == 0)
            def _():
                for r in range(ASTEPS):
                    dst[r] = jnp.zeros((LEV, 2 * W), f32)

            @pl.when(me_a == na - 1)
            def _():
                for r in range(ASTEPS):
                    dst[ROWS + ASTEPS + r] = jnp.zeros((LEV, 2 * W), f32)

    done.append(local(p0.at[pl.ds(ASTEPS, ROWS)], p_res, 11))

    arrive(h_e)
    g_gf.wait()
    spot = lax.rem(lane + 8, 24)
    from_left = (lane >= 64) & (lane < 112) & (spot < 6)
    from_right = (lane >= 64) & (lane < 112) & (spot >= 6) & (spot < 12)

    def strip(e, lefts, rights, n):
        place = 6 * (n % 4) + 48 * (n // 4)
        return jnp.where(from_left, rolled(lefts, 64 - place), jnp.where(from_right, rolled(rights, 70 - place), e))

    def strip_body(i, _):
        for n in range(0, 8, 4):
            made = []
            for h in range(n, n + 4):
                made.append(strip(own_e[8 * i + h], l_in[i], r_in[i], h))
            at = 4 * i + n // 2 + ASTEPS // 2 + 1
            put(sm, [at, at + 1], made, gf[...])
        return 0

    lax.fori_loop(0, ROWS // 8, strip_body, 0)
    for q in range(ASTEPS // 2):
        made = []
        for flat, first, corner, there in ((top_flat, 2, 0, me_a > 0), (bot_flat, 0, 2, me_a < na - 1)):
            for h in range(2):
                r = 2 * q + h if corner == 0 else ASTEPS - 2 - 2 * q + h
                e0, e1 = beside_row(flat, 0, r + first), beside_row(flat, 1, r + first)
                e = jnp.where((lane >= OWN) & (lane < 3 * OWN), rolled(e1, 2 * OWN), e0)
                z = strip(e, d_in[corner], d_in[corner + 1], r + first)
                made.append(jnp.where(there, z, 0.0))
        put(sm, [q + 1, PAIRS - q], made, gf[...], (ASTEPS - 2 * q - 1) // 2 * 2)
    s6[0] = jnp.zeros((LEV, 2 * W), f32)
    s6[PAIRS + 1] = jnp.zeros((LEV, 2 * W), f32)

    d_strip = jnp.broadcast_to(eig[kind, pl.ds(1, 1), :], (LEV, W))
    for k in range(ASTEPS - 1, -1, -1):
        ssrc, sdst = sm[k + 1], sm[k]
        first = ASTEPS - k

        def strip_step(i, _):
            q = i + first // 2
            a0, a1 = ssrc[q + 1, :, :W], ssrc[q + 1, :, W:]
            sdst[q + 1, :, :W] = sdst[q + 1, :, :W] + ((ssrc[q, :, W:] + a1) + d_strip * a0)
            sdst[q + 1, :, W:] = sdst[q + 1, :, W:] + ((ssrc[q + 2, :, :W] + a0) + d_strip * a1)
            return 0
        lax.fori_loop(0, PAIRS - 2 * (first // 2), strip_step, 0)

        if k:
            @pl.when(me_a == 0)
            def _():
                for r in range(ASTEPS // 2):
                    sdst[r + 1] = jnp.zeros((LEV, 2 * W), f32)

            @pl.when(me_a == na - 1)
            def _():
                for r in range(ASTEPS // 2):
                    sdst[(ROWS + ASTEPS) // 2 + r + 1] = jnp.zeros((LEV, 2 * W), f32)

    done.append(local(s0.at[pl.ds(ASTEPS // 2 + 1, ROWS // 2)], s_res, 12))

    p_in[mine_rows] = p_out[mine_rows]
    arrive(g_p)
    mine = pick(chosen_t, p_in[...])
    for k in range(4):
        x = mine[:, W * k:W * (k + 1)]
        hi = high(x)
        mx[pl.ds(k, BLK, stride=8), :] = hi
        mx[pl.ds(4 + k, BLK, stride=8), :] = x - hi
    g_down.wait()
    lax.fori_loop(0, BLK, lambda b, _: (remap(b, down_v, True), 0)[1], 0, unroll=4)
    for v in range(4):
        term[v] = cb[pl.ds(v, BLK, stride=8), :] * lf
    done.append(local(term, t_res, 13))

    arrive(h_f)
    rows48, lanes384 = rows_of((ROWS + 16, 3 * W)), lanes((ROWS + 16, 3 * W))
    grid_in = ((rows48 >= 8) | (me_a > 0)) & ((rows48 < ROWS + 8) | (me_a < na - 1))
    grid_in = grid_in & ((lanes384 >= W) | (me_o > 0)) & ((lanes384 < 2 * W) | (me_o < no - 1))
    grid_in = jnp.where(grid_in, 1.0, 0.0)
    for v in range(2):
        cur = jnp.concatenate([
            jnp.concatenate([fx_c[0, v], fx_t[v], fx_c[1, v]], 1),
            jnp.concatenate([fx_l[v], fx[v], fx_r[v]], 1),
            jnp.concatenate([fx_c[2, v], fx_b[v], fx_c[3, v]], 1),
        ], 0) * grid_in
        for j in range(8):
            if j == 7:
                gs[v, pl.ds(j, ROWS, stride=8), :] = jnp.zeros((ROWS, W), f32)
                break
            gs[v, pl.ds(j, ROWS, stride=8), :] = cur[8:8 + ROWS, W:2 * W]
            if j < 6:
                cur = grid_in * (
                    (rolled(cur, 1, 0) + rolled(cur, ROWS + 15, 0)) + (rolled(cur, 1) + rolled(cur, 3 * W - 1))
                )
    done.append(local(gs, g_res, 14))
    for c in sent:
        c.wait_send()
    for c in done:
        c.wait()


def finish(no, rows, tile, side, powers, wf, ocean, term, gain, qi, gi, air_out, ocean_out, flat):
    me_o = lax.axis_index("ocn")
    kind = jnp.where(me_o == 0, 1, jnp.where(me_o == no - 1, 2, 0))
    mids = changed([tile[x, :, W * v:W * (v + 1)] for x in range(rows) for v in range(2)], qi[...])
    hi, mid = parts2(jnp.concatenate([side[x // 2, :, W * (x % 2):W * (x % 2 + 1)] for x in range(rows)], 0))
    beside = mm(jnp.concatenate([hi, mid, hi], 1), gi[kind])
    for x in range(rows):
        g = jnp.concatenate([powers[v, 8 * x:8 * x + 8, :] for v in range(2)], 1)
        hi = high(g)
        rhs = jnp.concatenate([hi, g - hi, hi, jnp.zeros((8, 2 * W), f32)], 0).astype(bf16)
        extra = mm(wf[...], rhs)[:LEV] + beside[LEV * x:LEV * (x + 1)]
        for v in range(2):
            flat[pl.ds(v * LEV * rows + x, LEV, stride=rows), :] = mids[2 * x + v] + extra[:, W * v:W * (v + 1)]
    air_out[...] = flat[...].reshape(2 * LEV, rows, W)
    for n in range(4):
        ocean_out[n] = ocean[n] + gain[0, n] * term[0]


def shards(
    na, no,
    atm_state, ocn_state, land, ocn_kappa, partner, partner_row, remap_up, remap_down,
    surface_mix, drag, level_kappa, vertical_mix, depth_gain,
):
    cap = max(2, 2 * BLK // no)
    slots = no * cap
    vmem = pl.BlockSpec(memory_space=pltpu.VMEM)
    smem = pl.BlockSpec(memory_space=pltpu.SMEM)
    hbm = pl.BlockSpec(memory_space=pl.ANY)

    def v(*shape, dtype=f32):
        return pltpu.VMEM(shape, dtype)

    scratch = [
        v(2 * LEV * ROWS, W), v(2 * LEV, 8, W), v(2 * LEV, 8, W), v(2 * LEV * 8, W), v(2 * LEV * 8, W), v(16, BLK, W), v(BLK, W, W), v(BLK, W, W),
        v(ROWS, LEV, W), v(4, LEV, W), v(4, LEV, W), v(4, LEV, W), v(4, LEV, W), v(4, LEV, W),
        v(18, BLK, W), v(2, BLK, W), v(18, 8, W), v(18, 8, W), v(2, BLK, W), v(2, BLK, W), v(4, 2, 8, W),
        v(slots, W), v(slots, W), v(slots, 4 * W), v(slots, 4 * W), v(slots, 4 * W), v(slots, 4 * W),
        v(2, ROWS, W), v(2, ROWS, W), v(2, ROWS, W), v(2, 8, W), v(2, 8, W), v(4, 2, 8, W),
        v(BLK * 8, W), v(BLK * 8, W), v(512, 240, dtype=bf16), v(80, 32, dtype=bf16), v(2, ROWS * 8, W),
        v(16, BLK, W), v(4, BLK, W), v(4, BLK, W),
        v(2 * W, 2 * W, dtype=bf16), v(2 * W, 2 * W, dtype=bf16),
    ]
    scratch += [v(EXT, LEV, 2 * W) for _ in range(7)]
    scratch += [v(PAIRS + 2, LEV, 2 * W) for _ in range(7)]
    dma = pltpu.SemaphoreType.DMA
    scratch += [dma((15,)), dma((24,)), dma((24,)), dma((3, no)), dma((3, no))]
    q_there, q_back, g_there, g_back, eig = [jnp.asarray(m) for m in transforms()]

    def out(*shape, dtype=f32):
        return jax.ShapeDtypeStruct(shape, dtype)

    tile, side, powers, wf, ocean, term = pl.pallas_call(
        functools.partial(kernel, na, no, cap),
        out_shape=(
            out(ROWS, LEV, 2 * W), out(ROWS // 2, LEV, 2 * W), out(2, ROWS * 8, W), out(80, 32, dtype=bf16),
            out(16, BLK, W), out(4, BLK, W),
        ),
        in_specs=[hbm, hbm, hbm, vmem, vmem, vmem, vmem, hbm, hbm, smem, vmem, vmem, vmem, hbm, hbm, vmem],
        out_specs=(hbm,) * 6,
        scratch_shapes=scratch,
        compiler_params=pltpu.CompilerParams(
            collective_id=0, has_side_effects=True, vmem_limit_bytes=63 * 1024 * 1024
        ),
    )(
        atm_state.reshape(2 * LEV, ROWS, W),
        atm_state.reshape(2 * LEV * ROWS, W),
        ocn_state.reshape(16, BLK, W),
        land,
        ocn_kappa,
        partner.reshape(1, BLK),
        partner_row.reshape(1, BLK),
        remap_up,
        remap_down,
        surface_mix,
        drag,
        level_kappa.reshape(1, LEV),
        vertical_mix,
        q_there,
        g_there,
        eig,
    )
    rows = 8
    whole = pl.BlockSpec(memory_space=pltpu.VMEM)
    air, sea = pl.pallas_call(
        functools.partial(finish, no, rows),
        grid=(ROWS // rows,),
        out_shape=(out(2 * LEV, ROWS, W), out(16, BLK, W)),
        in_specs=[
            pl.BlockSpec((rows, LEV, 2 * W), lambda i: (i, 0, 0)),
            pl.BlockSpec((rows // 2, LEV, 2 * W), lambda i: (i, 0, 0)),
            pl.BlockSpec((2, rows * 8, W), lambda i: (0, i, 0)),
            whole,
            pl.BlockSpec((4, BLK, W), lambda i: (i, 0, 0)),
            pl.BlockSpec((1, BLK, W), lambda i: (i, 0, 0)),
            smem,
            whole,
            whole,
        ],
        out_specs=(
            pl.BlockSpec((2 * LEV, rows, W), lambda i: (0, i, 0)),
            pl.BlockSpec((4, BLK, W), lambda i: (i, 0, 0)),
        ),
        scratch_shapes=[v(2 * LEV * rows, W)],
        compiler_params=pltpu.CompilerParams(vmem_limit_bytes=63 * 1024 * 1024),
    )(tile, side, powers, wf, ocean, term, depth_gain.reshape(1, 4), q_back, g_back)
    return air.reshape(atm_state.shape), sea.reshape(ocn_state.shape)


def solution(mesh):
    placed = (
        P(None, None, "atm", "ocn"),
        P(None, None, "atm", "ocn"),
        P("atm", "ocn"),
        P("atm", "ocn"),
        P("ocn", "atm", None),
        P("ocn", "atm", None),
        P("atm", "ocn", None),
        P("atm", "ocn", None),
        P(),
        P("atm", "ocn"),
        P(),
        P(),
        P(),
    )
    return jax.shard_map(
        functools.partial(shards, mesh.shape["atm"], mesh.shape["ocn"]),
        mesh=mesh,
        in_specs=placed,
        out_specs=(P(None, None, "atm", "ocn"), P(None, None, "atm", "ocn")),
        check_vma=False,
    )
```

```python
import functools

import jax
import jax.numpy as jnp
import numpy as np
from jax import lax
from jax.experimental import pallas as pl
from jax.experimental.pallas import tpu as pltpu
from jax.sharding import PartitionSpec as P

f32 = jnp.float32
bf16 = jnp.bfloat16
LEV = 72
ASTEPS = 6
OSTEPS = 4
ROWS = 32
BLK = 64
W = 128
EXT = ROWS + 2 * ASTEPS
PAIRS = EXT // 2


def mm(a, b, dims=((1,), (0,)), precision=None):
    return lax.dot_general(a, b, (dims, ((), ())), precision=precision, preferred_element_type=f32)


def high(x):
    return x.astype(bf16).astype(f32)


def pick(onehot, x):
    left = onehot.astype(bf16)
    hi = high(x)
    rest = x - hi
    mid = high(rest)
    low = rest - mid
    return mm(left, hi.astype(bf16)) + mm(left, mid.astype(bf16)) + mm(left, low.astype(bf16))


def lanes(shape):
    return lax.broadcasted_iota(jnp.int32, shape, len(shape) - 1)


def rows_of(shape):
    return lax.broadcasted_iota(jnp.int32, shape, len(shape) - 2)


def rolled(x, shift, axis=1):
    if isinstance(shift, int):
        shift = shift % x.shape[axis]
        if shift == 0:
            return x
    return pltpu.roll(x, shift, axis)


def parts2(x):
    hi = x.astype(bf16)
    return hi, (x - hi.astype(f32)).astype(bf16)


def changed(rows, matrix):
    res = mm(jnp.concatenate(parts2(jnp.concatenate(rows, 0)), 1), matrix)
    res = res[:, :W] + res[:, W:]
    return [res[LEV * n:LEV * (n + 1)] for n in range(len(rows))]


SEG = 3 * ASTEPS
OWN = 2 * ASTEPS


def sines(n):
    k = np.arange(1, n + 1)
    return np.sqrt(2.0 / (n + 1)) * np.sin(np.pi * np.outer(k, k) / (n + 1)), 2.0 * np.cos(np.pi * k / (n + 1))


def two_parts(m):
    hi = np.asarray(m, np.float32).astype(jnp.bfloat16)
    mid = (np.asarray(m, np.float64) - hi.astype(np.float64)).astype(np.float32).astype(jnp.bfloat16)
    return hi, mid


def wide_parts(m):
    hi, mid = two_parts(m)
    return np.concatenate([np.concatenate([hi, mid], 1), np.concatenate([hi, np.zeros_like(mid)], 1)], 0)


def transforms():
    q, d = sines(W)
    back = q.copy()
    back[:, :ASTEPS] = 0.0
    back[:, W - ASTEPS:] = 0.0
    gf, gi, ds = [], [], []
    for kind in range(3):
        there, again, eig = np.zeros((W, W)), np.zeros((W, 2 * W)), np.zeros((1, W))
        for seg in range(4):
            var, side = divmod(seg, 2)
            places = list(range(SEG))
            if kind == 1 and side == 0:
                places = places[ASTEPS:]
            if kind == 2 and side == 1:
                places = places[:OWN]
            basis, values = sines(len(places))
            for n, place in enumerate(places):
                col = place - ASTEPS if side == 0 else W - OWN + place
                if col < 0:
                    lane = 64 + 24 * var + col + ASTEPS
                elif col >= W:
                    lane = 70 + 24 * var + col - W
                else:
                    lane = (col + 24 * var) % W
                there[lane, SEG * seg:SEG * seg + len(places)] = basis[n]
                if ASTEPS <= place < OWN:
                    again[SEG * seg:SEG * seg + len(places), W * var + col] = basis[:, n]
            eig[0, SEG * seg:SEG * seg + len(places)] = values
        gf.append(wide_parts(there))
        hi, mid = two_parts(again)
        gi.append(np.concatenate([hi, hi, mid], 0))
        ds.append(np.concatenate([d.reshape(1, W), eig] + [np.zeros((1, W))] * 6, 0))
    return wide_parts(q), wide_parts(back), np.stack(gf), np.stack(gi), np.stack(ds).astype(np.float32)


def kernel(
    na, no, cap,
    atm, atm_flat, ocn, land, kappa, partner, prow, up, down, smix, drag, lk, vm, qf_all, gf_all, eig,
    p_res, s_res, g_res, w_res, u_res, t_res,
    a_flat, a_top, a_bot, top_flat, bot_flat, u_own, up_v, down_v,
    own_e, r_out, l_out, l_in, r_in, d_in,
    ob, oe, ob_top, ob_bot, oe_l, oe_r, oe_c,
    rid_out, rid_in, c_out, c_in, p_out, p_in,
    fx, fx_l, fx_r, fx_t, fx_b, fx_c,
    mx, cb, w_s, wf_s, gs, us, st, term, qf, gf,
    p0, p1, p2, p3, p4, p5, p6,
    s0, s1, s2, s3, s4, s5, s6,
    loc, hs, hr, ps, pr,
):
    me_a = lax.axis_index("atm")
    me_o = lax.axis_index("ocn")
    above, below = lax.rem(me_a + na - 1, na), lax.rem(me_a + 1, na)
    left, right = lax.rem(me_o + no - 1, no), lax.rem(me_o + 1, no)
    slots = no * cap
    pm = (p0, p1, p2, p3, p4, p5, p6)
    sm = (s0, s1, s2, s3, s4, s5, s6)

    def local(src, dst, i):
        c = pltpu.make_async_copy(src, dst, loc.at[i])
        c.start()
        return c

    g_ocn = local(ocn, u_own, 0)
    chunks = 4
    part = BLK // chunks
    g_up = [local(up.at[pl.ds(i * part, part)], up_v.at[pl.ds(i * part, part)], 1 + i) for i in range(chunks)]
    g_atm = local(atm_flat, a_flat, 5)
    kind = jnp.where(me_o == 0, 1, jnp.where(me_o == no - 1, 2, 0))
    g_qf = local(qf_all, qf, 7)

    barrier = pltpu.get_barrier_semaphore()
    greeted = [(me_a, lax.rem(me_o + d, no)) for d in range(1, no)]
    greeted += [(r, c) for r in (above, below) for c in (me_o, left, right)]
    for r, c in greeted:
        pl.semaphore_signal(barrier, inc=1, device_id={"atm": r, "ocn": c}, device_id_type=pl.DeviceIdType.MESH)
    pl.semaphore_wait(barrier, len(greeted))

    sent = []
    lane = lanes((LEV, W))

    def send(src, dst, i, r, c):
        d = pltpu.make_async_remote_copy(
            src_ref=src, dst_ref=dst, send_sem=hs.at[i], recv_sem=hr.at[i],
            device_id={"atm": r, "ocn": c}, device_id_type=pl.DeviceIdType.MESH,
        )
        d.start()
        sent.append(d)
        return d

    def spread(src, dst, group):
        made = []
        for d in range(1, no):
            peer = lax.rem(me_o + d, no)
            c = pltpu.make_async_remote_copy(
                src_ref=src.at[pl.ds(pl.multiple_of(peer * cap, 8), cap)],
                dst_ref=dst.at[pl.ds(pl.multiple_of(me_o * cap, 8), cap)],
                send_sem=ps.at[group, d], recv_sem=pr.at[group, d],
                device_id={"atm": me_a, "ocn": peer}, device_id_type=pl.DeviceIdType.MESH,
            )
            c.start()
            sent.append(c)
            made.append(c)
        return made

    def arrive(made):
        for c in made:
            c.wait_recv()

    mine_rows = pl.ds(pl.multiple_of(me_o * cap, 8), cap)

    lf = land[...].astype(f32)
    g_ocn.wait()
    for c in range(16):
        ob[c] = u_own[c]
    ob[16] = lf
    ob[17] = kappa[...]
    lane64 = lanes((BLK, W))
    edge = jnp.zeros((BLK, W), f32)
    for c in range(16):
        edge = jnp.where(lane64 // 8 == c, rolled(u_own[c], 8 * c + 4), edge)
    oe[0] = edge
    oe[1] = jnp.where(lane64 // 8 == 0, rolled(lf, 4), rolled(kappa[...], 12))
    h_ob = [
        send(ob.at[:, pl.ds(0, 8)], ob_bot, 2, above, me_o),
        send(ob.at[:, pl.ds(BLK - 8, 8)], ob_top, 3, below, me_o),
        send(oe, oe_r, 4, me_a, left),
        send(oe, oe_l, 5, me_a, right),
        send(oe.at[:, pl.ds(BLK - 8, 8)], oe_c.at[0], 6, below, right),
        send(oe.at[:, pl.ds(BLK - 8, 8)], oe_c.at[1], 7, below, left),
        send(oe.at[:, pl.ds(0, 8)], oe_c.at[2], 8, above, right),
        send(oe.at[:, pl.ds(0, 8)], oe_c.at[3], 9, above, left),
    ]

    h_bot = send(atm.at[:, pl.ds(0, 8)], a_bot, 0, above, me_o)
    h_top = send(atm.at[:, pl.ds(ROWS - 8, 8)], a_top, 1, below, me_o)

    t_row = partner[...].astype(f32)
    r_row = prow[...].astype(f32)
    ii, jj = rows_of((BLK, BLK)), lanes((BLK, BLK))
    t_all = jnp.broadcast_to(t_row, (BLK, BLK))
    t_col = jnp.sum(jnp.where(ii == jj, t_all, 0.0), axis=1, keepdims=True)
    same = t_col == t_all
    pos_row = jnp.sum(jnp.where(same & (ii < jj), 1.0, 0.0), axis=0, keepdims=True)
    pos_col = jnp.sum(jnp.where(same & (jj < ii), 1.0, 0.0), axis=1, keepdims=True)
    slot_row = t_row * cap + pos_row
    slot_col = t_col * cap + pos_col
    chosen = jnp.where(rows_of((slots, BLK)).astype(f32) == slot_row, 1.0, 0.0)
    chosen_t = jnp.where(lanes((BLK, slots)).astype(f32) == slot_col, 1.0, 0.0)
    rid = jnp.sum(chosen * (r_row + 1.0), axis=1, keepdims=True) - 1.0
    rid_out[...] = jnp.broadcast_to(rid, (slots, W))
    g_rid = spread(rid_out, rid_in, 0)

    exact = lax.Precision.HIGHEST
    rate = lk[...]
    zpad = jnp.zeros((LEV, W - LEV), f32)
    ca = jnp.concatenate([vm[...] * (1.0 - 4.0 * rate), zpad], 1)
    cc = jnp.concatenate([vm[...] * rate, zpad], 1)
    lhs = jnp.concatenate([ca, cc], 0)[:, :LEV]
    q = mm(lhs, jnp.concatenate([ca, cc], 1), precision=exact)
    q0, q1, q2 = q[:LEV, :W], q[:LEV, W:] + q[LEV:, :W], q[LEV:, W:]
    t = mm(lhs, jnp.concatenate([q0, q1, q2], 1), precision=exact)
    cubes = (
        t[:LEV, :W],
        t[:LEV, W:2 * W] + t[LEV:, :W],
        t[:LEV, 2 * W:] + t[LEV:, W:2 * W],
        t[LEV:, 2 * W:],
    )
    t = mm(jnp.concatenate(cubes, 0)[:, :LEV], jnp.concatenate(cubes, 1), precision=exact)
    wide = []
    column = jnp.zeros((LEV, W), f32)
    for k in range(7):
        m = None
        for i in range(max(0, k - 3), min(3, k) + 1):
            piece = t[LEV * i:LEV * (i + 1), W * (k - i):W * (k - i + 1)]
            m = piece if m is None else m + piece
        hi = high(m)
        z = jnp.zeros((LEV, W), f32)
        hi2 = jnp.concatenate([hi, z], 1)
        wide.append(hi2 + rolled(hi2, 80) + rolled(jnp.concatenate([m - hi, z], 1), 160))
        column = jnp.where(lane == k, rolled(m, k - (LEV - 1)), column)
    wide.append(jnp.zeros((8, 2 * W), f32))
    w_s[...] = jnp.concatenate(wide, 0)[:, :240].astype(bf16)
    chi = high(column)
    wf = chi + rolled(chi, 8) + rolled(column - chi, 16)
    wf_s[...] = jnp.concatenate([wf, jnp.zeros((8, W), f32)], 0)[:, :32].astype(bf16)
    done = [local(wf_s, w_res, 9)]

    for k in range(4):
        total = smix[k, 0] * u_own[0]
        for c in range(1, 16):
            total = total + smix[k, c] * u_own[c]
        total = total * lf
        hi = high(total)
        mx[pl.ds(k, BLK, stride=8), :] = hi
        mx[pl.ds(4 + k, BLK, stride=8), :] = total - hi

    def remap(b, weights, transposed):
        block = weights[b]
        hi = high(block)
        parts = (hi.astype(bf16), (block - hi).astype(bf16))
        vec = mx[pl.ds(pl.multiple_of(b * 8, 8), 8), :].astype(bf16)
        if transposed:
            res = mm(vec, jnp.concatenate(parts, 0), ((1,), (1,)))
        else:
            res = mm(vec, jnp.concatenate(parts, 1))
        first = res[:, :W]
        cb[pl.ds(pl.multiple_of(b * 8, 8), 8), :] = first + rolled(first, 4, 0) + res[:, W:]

    def own_row(v, x):
        return a_flat[pl.ds(v * LEV * ROWS + x, LEV, stride=ROWS), :]

    def gather(g, _):
        to_r = to_l = jnp.zeros((LEV, W), f32)
        for n in range(8):
            x = 8 * g + n
            e = jnp.where((lane >= OWN) & (lane < 3 * OWN), rolled(own_row(1, x), 2 * OWN), own_row(0, x))
            own_e[x] = e
            place = 6 * (n % 4) + 48 * (n // 4)
            here = (lane // 48 == n // 4) & (lax.rem(lane, 24) // 6 == n % 4)
            to_r = jnp.where(here, rolled(e, place + 6), to_r)
            to_l = jnp.where(here, rolled(e, place), to_l)
        r_out[g] = to_r
        l_out[g] = to_l

    def gather_remap(g, _):
        for n in range(16):
            remap(16 * g + n, up_v, False)
        gather(g, _)
        return 0

    for i in range(chunks):
        g_up[i].wait()
    g_atm.wait()
    lax.fori_loop(0, 4, gather_remap, 0)
    g_gf = local(gf_all.at[kind], gf, 8)
    g_down = local(down, down_v, 6)
    fields = jnp.concatenate([cb[pl.ds(k, BLK, stride=8), :] for k in range(4)], 1)
    c_out[...] = pick(chosen, fields)
    g_c = spread(c_out, c_in, 1)


    h_e = [
        send(r_out, l_in, 10, me_a, right),
        send(l_out, r_in, 11, me_a, left),
        send(r_out.at[3], d_in.at[0], 12, below, right),
        send(l_out.at[3], d_in.at[1], 13, below, left),
        send(r_out.at[0], d_in.at[2], 14, above, right),
        send(l_out.at[0], d_in.at[3], 15, above, left),
    ]

    def powers(x, low=0):
        hi = high(x)
        z = jnp.zeros((8, 2 * W), f32)
        h = jnp.concatenate([hi, z], 0).astype(bf16)
        m = jnp.concatenate([x - hi, z], 0).astype(bf16)
        return mm(w_s[pl.ds(LEV * low, 512 - LEV * low), :], jnp.concatenate([h, m, h], 0))

    def put(refs, places, rows, matrix, low=0):
        turned = changed(rows, matrix)
        for n, place in enumerate(places):
            res = powers(jnp.concatenate(turned[2 * n:2 * n + 2], 1), low)
            for k in range(low, 7):
                refs[k][place] = res[LEV * (k - low):LEV * (k - low + 1)]

    arrive(h_ob)
    tall = BLK + 16
    rr = rows_of((tall, W))
    row_in = ((rr >= 8) | (me_a > 0)) & ((rr < BLK + 8) | (me_a < na - 1))
    lane_t = lanes((tall, W))

    def tall_of(c):
        return jnp.concatenate([ob_top[c], ob[c], ob_bot[c]], 0)

    def tall_edge(n, side):
        body = oe_l[n] if side == 0 else oe_r[n]
        return jnp.concatenate([oe_c[side, n], body, oe_c[2 + side, n]], 0)

    def neighbours(x):
        return (rolled(x, 1, 0) + rolled(x, tall - 1, 0)) + (rolled(x, 1) + rolled(x, W - 1))

    def stepped(x, c0, c1):
        for _ in range(OSTEPS):
            x = c0 * x + c1 * neighbours(x)
        return x

    sea = jnp.where(row_in, tall_of(16), 0.0)
    kap = tall_of(17)
    c1 = kap * sea
    c0 = sea - c1 * neighbours(sea)

    def edges(own, l_edge, r_edge, at, slot):
        out = jnp.where(lane_t < 32 * slot + 4, rolled(l_edge, 32 * slot - at), rolled(own, 32 * slot + 4))
        out = jnp.where(lane_t >= 32 * slot + 16, rolled(own, 32 * slot + 24), out)
        return jnp.where(lane_t >= 32 * slot + 24, rolled(r_edge, 32 * slot + 20 - at), out)

    in_l = (lane_t >= 4) | (me_o > 0)
    in_r = (lane_t < 24) | (me_o < no - 1)
    used = ((lane_t < 12) | ((lane_t >= 16) & (lane_t < 28))) & in_l & in_r & row_in
    tl, tr = tall_edge(1, 0), tall_edge(1, 1)
    e_sea = jnp.where(used, edges(tall_of(16), tl, tr, 0, 0), 0.0)
    e_kap = jnp.where(used, edges(kap, tl, tr, 8, 0), 0.0)

    def four(x):
        return (x + rolled(x, 32)) + (rolled(x, 64) + rolled(x, 96))

    e_sea, e_kap = four(e_sea), four(e_kap)
    e1 = e_kap * e_sea
    e0 = e_sea - e1 * neighbours(e_sea)
    ul, ur = tall_edge(0, 0), tall_edge(0, 1)
    for g in range(4):
        total = edges(tall_of(4 * g), ul, ur, 32 * g, 0)
        for s in range(1, 4):
            c = 4 * g + s
            total = jnp.where(lane_t >= 32 * s, edges(tall_of(c), ul, ur, 8 * c, s), total)
        st[g] = stepped(e_sea * total, e0, e1)[8:8 + BLK]

    def channel(c, e, slot):
        mid = stepped(sea * tall_of(c), c0, c1)[8:8 + BLK]
        mid = jnp.where(lane64 < 4, rolled(e, lax.rem(2 * W - 32 * slot - 4, W)), mid)
        mid = jnp.where(lane64 >= W - 4, rolled(e, lax.rem(W + 104 - 32 * slot, W)), mid)
        us[c] = mid + (1.0 - lf) * u_own[c]

    g_qf.wait()

    def own_body(i, _):
        xs = [4 * i + n for n in range(4)]
        put(pm, [x + ASTEPS for x in xs], [own_row(v, x) for x in xs for v in range(2)], qf[...])
        for h in range(2):
            slot = 2 * lax.rem(i, 2) + h
            channel(2 * i + h, st[lax.div(i, 2)], slot)
        return 0

    lax.fori_loop(0, ROWS // 4, own_body, 0, unroll=4)

    done.append(local(us, u_res, 10))

    rid_in[mine_rows] = rid_out[mine_rows]
    c_in[mine_rows] = c_out[mine_rows]
    arrive(g_rid)
    place_t = jnp.where(rid_in[...] == lanes((slots, W)).astype(f32), 1.0, 0.0)
    place = place_t.T[:ROWS]
    arrive(g_c)
    mixed = pick(place, c_in[...])
    flux = []
    for k in range(4):
        flux.append(drag[...] * (mixed[:, W * k:W * (k + 1)] - a_flat[pl.ds(((k % 2) * LEV + LEV - 1) * ROWS, ROWS), :]))
    p_out[...] = pick(place_t[:, :ROWS], jnp.concatenate(flux, 1))
    g_p = spread(p_out, p_in, 2)
    fx[0] = flux[0]
    fx[1] = flux[1]
    h_f = [
        send(fx, fx_r, 16, me_a, left),
        send(fx, fx_l, 17, me_a, right),
        send(fx.at[:, pl.ds(0, 8)], fx_b, 18, above, me_o),
        send(fx.at[:, pl.ds(ROWS - 8, 8)], fx_t, 19, below, me_o),
        send(fx.at[:, pl.ds(ROWS - 8, 8)], fx_c.at[0], 20, below, right),
        send(fx.at[:, pl.ds(ROWS - 8, 8)], fx_c.at[1], 21, below, left),
        send(fx.at[:, pl.ds(0, 8)], fx_c.at[2], 22, above, right),
        send(fx.at[:, pl.ds(0, 8)], fx_c.at[3], 23, above, left),
    ]

    h_top.wait_recv()
    h_bot.wait_recv()

    top_flat[...] = jnp.where(me_a > 0, a_top[...], 0.0).reshape(2 * LEV * 8, W)
    bot_flat[...] = jnp.where(me_a < na - 1, a_bot[...], 0.0).reshape(2 * LEV * 8, W)

    def beside_row(flat, v, x):
        return flat[pl.ds(v * LEV * 8 + x, LEV, stride=8), :]

    for r in range(ASTEPS):
        put(
            pm, [r, EXT - 1 - r],
            [beside_row(top_flat, v, r + 2) for v in range(2)]
            + [beside_row(bot_flat, v, ASTEPS - 1 - r) for v in range(2)],
            qf[...], (ASTEPS - r) // 2 * 2,
        )

    d_main = jnp.broadcast_to(eig[0, pl.ds(0, 1), :], (LEV, W))
    for k in range(ASTEPS - 1, -1, -1):
        src, dst = pm[k + 1], pm[k]
        first = ASTEPS - k
        count = EXT - 2 * first
        group = 4 if count % 4 == 0 else 2

        def main_body(i, _):
            r = first + i * group
            for h in range(2):
                sl = slice(W * h, W * (h + 1))
                near = [src[r - 1 + n, :, sl] for n in range(group + 2)]
                made = []
                for n in range(group):
                    c = near[n + 1]
                    made.append(dst[r + n, :, sl] + ((near[n] + near[n + 2]) + d_main * c))
                for n in range(group):
                    dst[r + n, :, sl] = made[n]
            return 0
        lax.fori_loop(0, count // group, main_body, 0, unroll=2 if count // group % 2 == 0 else 1)

        if k:
            @pl.when(me_a == 0)
            def _():
                for r in range(ASTEPS):
                    dst[r] = jnp.zeros((LEV, 2 * W), f32)

            @pl.when(me_a == na - 1)
            def _():
                for r in range(ASTEPS):
                    dst[ROWS + ASTEPS + r] = jnp.zeros((LEV, 2 * W), f32)

    done.append(local(p0.at[pl.ds(ASTEPS, ROWS)], p_res, 11))

    arrive(h_e)
    g_gf.wait()
    spot = lax.rem(lane + 8, 24)
    from_left = (lane >= 64) & (lane < 112) & (spot < 6)
    from_right = (lane >= 64) & (lane < 112) & (spot >= 6) & (spot < 12)

    def strip(e, lefts, rights, n):
        place = 6 * (n % 4) + 48 * (n // 4)
        return jnp.where(from_left, rolled(lefts, 64 - place), jnp.where(from_right, rolled(rights, 70 - place), e))

    def strip_body(i, _):
        for n in range(0, 8, 4):
            made = []
            for h in range(n, n + 4):
                made.append(strip(own_e[8 * i + h], l_in[i], r_in[i], h))
            at = 4 * i + n // 2 + ASTEPS // 2 + 1
            put(sm, [at, at + 1], made, gf[...])
        return 0

    lax.fori_loop(0, ROWS // 8, strip_body, 0, unroll=2)
    for q in range(ASTEPS // 2):
        made = []
        for flat, first, corner, there in ((top_flat, 2, 0, me_a > 0), (bot_flat, 0, 2, me_a < na - 1)):
            for h in range(2):
                r = 2 * q + h if corner == 0 else ASTEPS - 2 - 2 * q + h
                e0, e1 = beside_row(flat, 0, r + first), beside_row(flat, 1, r + first)
                e = jnp.where((lane >= OWN) & (lane < 3 * OWN), rolled(e1, 2 * OWN), e0)
                z = strip(e, d_in[corner], d_in[corner + 1], r + first)
                made.append(jnp.where(there, z, 0.0))
        put(sm, [q + 1, PAIRS - q], made, gf[...], (ASTEPS - 2 * q - 1) // 2 * 2)
    s6[0] = jnp.zeros((LEV, 2 * W), f32)
    s6[PAIRS + 1] = jnp.zeros((LEV, 2 * W), f32)

    d_strip = jnp.broadcast_to(eig[kind, pl.ds(1, 1), :], (LEV, W))
    for k in range(ASTEPS - 1, -1, -1):
        ssrc, sdst = sm[k + 1], sm[k]
        first = ASTEPS - k

        def strip_step(i, _):
            q = i + first // 2
            a0, a1 = ssrc[q + 1, :, :W], ssrc[q + 1, :, W:]
            sdst[q + 1, :, :W] = sdst[q + 1, :, :W] + ((ssrc[q, :, W:] + a1) + d_strip * a0)
            sdst[q + 1, :, W:] = sdst[q + 1, :, W:] + ((ssrc[q + 2, :, :W] + a0) + d_strip * a1)
            return 0
        lax.fori_loop(0, PAIRS - 2 * (first // 2), strip_step, 0, unroll=2)

        if k:
            @pl.when(me_a == 0)
            def _():
                for r in range(ASTEPS // 2):
                    sdst[r + 1] = jnp.zeros((LEV, 2 * W), f32)

            @pl.when(me_a == na - 1)
            def _():
                for r in range(ASTEPS // 2):
                    sdst[(ROWS + ASTEPS) // 2 + r + 1] = jnp.zeros((LEV, 2 * W), f32)

    done.append(local(s0.at[pl.ds(ASTEPS // 2 + 1, ROWS // 2)], s_res, 12))

    p_in[mine_rows] = p_out[mine_rows]
    arrive(g_p)
    mine = pick(chosen_t, p_in[...])
    for k in range(4):
        x = mine[:, W * k:W * (k + 1)]
        hi = high(x)
        mx[pl.ds(k, BLK, stride=8), :] = hi
        mx[pl.ds(4 + k, BLK, stride=8), :] = x - hi
    g_down.wait()
    lax.fori_loop(0, BLK, lambda b, _: (remap(b, down_v, True), 0)[1], 0, unroll=16)
    for v in range(4):
        term[v] = cb[pl.ds(v, BLK, stride=8), :] * lf
    done.append(local(term, t_res, 13))

    arrive(h_f)
    rows48, lanes384 = rows_of((ROWS + 16, 3 * W)), lanes((ROWS + 16, 3 * W))
    grid_in = ((rows48 >= 8) | (me_a > 0)) & ((rows48 < ROWS + 8) | (me_a < na - 1))
    grid_in = grid_in & ((lanes384 >= W) | (me_o > 0)) & ((lanes384 < 2 * W) | (me_o < no - 1))
    grid_in = jnp.where(grid_in, 1.0, 0.0)
    for v in range(2):
        cur = jnp.concatenate([
            jnp.concatenate([fx_c[0, v], fx_t[v], fx_c[1, v]], 1),
            jnp.concatenate([fx_l[v], fx[v], fx_r[v]], 1),
            jnp.concatenate([fx_c[2, v], fx_b[v], fx_c[3, v]], 1),
        ], 0) * grid_in
        for j in range(8):
            if j == 7:
                gs[v, pl.ds(j, ROWS, stride=8), :] = jnp.zeros((ROWS, W), f32)
                break
            gs[v, pl.ds(j, ROWS, stride=8), :] = cur[8:8 + ROWS, W:2 * W]
            if j < 6:
                cur = grid_in * (
                    (rolled(cur, 1, 0) + rolled(cur, ROWS + 15, 0)) + (rolled(cur, 1) + rolled(cur, 3 * W - 1))
                )
    done.append(local(gs, g_res, 14))
    for c in sent:
        c.wait_send()
    for c in done:
        c.wait()


def finish(no, rows, tile, side, powers, wf, ocean, term, gain, qi, gi, air_out, ocean_out, flat):
    me_o = lax.axis_index("ocn")
    kind = jnp.where(me_o == 0, 1, jnp.where(me_o == no - 1, 2, 0))
    mids = changed([tile[x, :, W * v:W * (v + 1)] for x in range(rows) for v in range(2)], qi[...])
    hi, mid = parts2(jnp.concatenate([side[x // 2, :, W * (x % 2):W * (x % 2 + 1)] for x in range(rows)], 0))
    beside = mm(jnp.concatenate([hi, mid, hi], 1), gi[kind])
    for x in range(rows):
        g = jnp.concatenate([powers[v, 8 * x:8 * x + 8, :] for v in range(2)], 1)
        hi = high(g)
        rhs = jnp.concatenate([hi, g - hi, hi, jnp.zeros((8, 2 * W), f32)], 0).astype(bf16)
        extra = mm(wf[...], rhs)[:LEV] + beside[LEV * x:LEV * (x + 1)]
        for v in range(2):
            flat[pl.ds(v * LEV * rows + x, LEV, stride=rows), :] = mids[2 * x + v] + extra[:, W * v:W * (v + 1)]
    air_out[...] = flat[...].reshape(2 * LEV, rows, W)
    for n in range(16 * rows // ROWS):
        ocean_out[n] = ocean[n] + gain[0, n % 4] * term[n // 4]


def shards(
    na, no,
    atm_state, ocn_state, land, ocn_kappa, partner, partner_row, remap_up, remap_down,
    surface_mix, drag, level_kappa, vertical_mix, depth_gain,
):
    cap = max(2, 2 * BLK // no)
    slots = no * cap
    vmem = pl.BlockSpec(memory_space=pltpu.VMEM)
    smem = pl.BlockSpec(memory_space=pltpu.SMEM)
    hbm = pl.BlockSpec(memory_space=pl.ANY)

    def v(*shape, dtype=f32):
        return pltpu.VMEM(shape, dtype)

    scratch = [
        v(2 * LEV * ROWS, W), v(2 * LEV, 8, W), v(2 * LEV, 8, W), v(2 * LEV * 8, W), v(2 * LEV * 8, W), v(16, BLK, W), v(BLK, W, W), v(BLK, W, W),
        v(ROWS, LEV, W), v(4, LEV, W), v(4, LEV, W), v(4, LEV, W), v(4, LEV, W), v(4, LEV, W),
        v(18, BLK, W), v(2, BLK, W), v(18, 8, W), v(18, 8, W), v(2, BLK, W), v(2, BLK, W), v(4, 2, 8, W),
        v(slots, W), v(slots, W), v(slots, 4 * W), v(slots, 4 * W), v(slots, 4 * W), v(slots, 4 * W),
        v(2, ROWS, W), v(2, ROWS, W), v(2, ROWS, W), v(2, 8, W), v(2, 8, W), v(4, 2, 8, W),
        v(BLK * 8, W), v(BLK * 8, W), v(512, 240, dtype=bf16), v(80, 32, dtype=bf16), v(2, ROWS * 8, W),
        v(16, BLK, W), v(4, BLK, W), v(4, BLK, W),
        v(2 * W, 2 * W, dtype=bf16), v(2 * W, 2 * W, dtype=bf16),
    ]
    scratch += [v(EXT, LEV, 2 * W) for _ in range(7)]
    scratch += [v(PAIRS + 2, LEV, 2 * W) for _ in range(7)]
    dma = pltpu.SemaphoreType.DMA
    scratch += [dma((15,)), dma((24,)), dma((24,)), dma((3, no)), dma((3, no))]
    q_there, q_back, g_there, g_back, eig = [jnp.asarray(m) for m in transforms()]

    def out(*shape, dtype=f32):
        return jax.ShapeDtypeStruct(shape, dtype)

    tile, side, powers, wf, ocean, term = pl.pallas_call(
        functools.partial(kernel, na, no, cap),
        out_shape=(
            out(ROWS, LEV, 2 * W), out(ROWS // 2, LEV, 2 * W), out(2, ROWS * 8, W), out(80, 32, dtype=bf16),
            out(16, BLK, W), out(4, BLK, W),
        ),
        in_specs=[hbm, hbm, hbm, vmem, vmem, vmem, vmem, hbm, hbm, smem, vmem, vmem, vmem, hbm, hbm, vmem],
        out_specs=(hbm,) * 6,
        scratch_shapes=scratch,
        compiler_params=pltpu.CompilerParams(
            collective_id=0, has_side_effects=True, vmem_limit_bytes=63 * 1024 * 1024
        ),
    )(
        atm_state.reshape(2 * LEV, ROWS, W),
        atm_state.reshape(2 * LEV * ROWS, W),
        ocn_state.reshape(16, BLK, W),
        land,
        ocn_kappa,
        partner.reshape(1, BLK),
        partner_row.reshape(1, BLK),
        remap_up,
        remap_down,
        surface_mix,
        drag,
        level_kappa.reshape(1, LEV),
        vertical_mix,
        q_there,
        g_there,
        eig,
    )
    rows = 16
    whole = pl.BlockSpec(memory_space=pltpu.VMEM)
    air, sea = pl.pallas_call(
        functools.partial(finish, no, rows),
        grid=(ROWS // rows,),
        out_shape=(out(2 * LEV, ROWS, W), out(16, BLK, W)),
        in_specs=[
            pl.BlockSpec((rows, LEV, 2 * W), lambda i: (i, 0, 0)),
            pl.BlockSpec((rows // 2, LEV, 2 * W), lambda i: (i, 0, 0)),
            pl.BlockSpec((2, rows * 8, W), lambda i: (0, i, 0)),
            whole,
            pl.BlockSpec((16 * rows // ROWS, BLK, W), lambda i: (i, 0, 0)),
            pl.BlockSpec((4 * rows // ROWS, BLK, W), lambda i: (i, 0, 0)),
            smem,
            whole,
            whole,
        ],
        out_specs=(
            pl.BlockSpec((2 * LEV, rows, W), lambda i: (0, i, 0)),
            pl.BlockSpec((16 * rows // ROWS, BLK, W), lambda i: (i, 0, 0)),
        ),
        scratch_shapes=[v(2 * LEV * rows, W)],
        compiler_params=pltpu.CompilerParams(vmem_limit_bytes=63 * 1024 * 1024),
    )(tile, side, powers, wf, ocean, term, depth_gain.reshape(1, 4), q_back, g_back)
    return air.reshape(atm_state.shape), sea.reshape(ocn_state.shape)


def solution(mesh):
    placed = (
        P(None, None, "atm", "ocn"),
        P(None, None, "atm", "ocn"),
        P("atm", "ocn"),
        P("atm", "ocn"),
        P("ocn", "atm", None),
        P("ocn", "atm", None),
        P("atm", "ocn", None),
        P("atm", "ocn", None),
        P(),
        P("atm", "ocn"),
        P(),
        P(),
        P(),
    )
    return jax.shard_map(
        functools.partial(shards, mesh.shape["atm"], mesh.shape["ocn"]),
        mesh=mesh,
        in_specs=placed,
        out_specs=(P(None, None, "atm", "ocn"), P(None, None, "atm", "ocn")),
        check_vma=False,
    )
```
